256 devices in a mesh: blk: 32 (over z, y_hi, core), rep: 8 (over x, y_lo).
Axes of the slice: x: 4, y: 4 (y_hi: 2, y_lo: 2; y = y_hi * 2 + y_lo), z: 8, core: 2. Of those that a mesh axis runs over, the one named last changes fastest.
Arguments:
- features: bfloat16 [32768, 512], P('blk'), may hold values from -6 to 6
- layer_weight: bfloat16 [512, 512], replicated, may hold values from -0.25 to 0.25
- adjacency_tiles: bfloat16 [32, 32, 8, 128, 128], P('blk', 'rep'), may hold values from -0.125 to 0.125
- tile_slots: int32 [32, 32, 8], P('blk', 'rep'), may hold values from 0 to 63, as said below
- tile_counts: int32 [32, 32], P('blk', 'rep'), may hold values from 1 to 8, as said below
- cotangent: bfloat16 [32768, 512], P('blk'), may hold values from -6 to 6
Outputs:
- activated: bfloat16 [32768, 512], P('blk')
- grad_input: bfloat16 [32768, 512], P('blk')
- grad_weight: float32 [512, 512], replicated
The draws below stay inside these ranges and needn't reach their ends.
Inputs may be any that keep to these rules, and one draw needn't show every extreme that they name: `tile_slots`: the 8 entries of one list are distinct; entry v names row tile v // 8 and column tile v % 8. Only the first tile_counts[b, j] entries of list (b, j) are live; some list is full.
All inputs are finite; a program needn't handle non-finite values.
Results may differ from the reference program's by a relative error of at most 0.0065.
Values may be sent and summed in bfloat16 or wider, within the bound.
A program may use at most 64 MiB of HBM per device.

```python
import math
import jax
import jax.numpy as jnp
from jax import lax

FEATURES = 512
TILE = 128
TILES = 8
SLOTS = 8
STEPS = 4
NODES = 32768
N_BLK = 32


def draw_tile_slots(key, part):
    key = jax.random.fold_in(key, 7)
    many_keys = jax.random.split(key, N_BLK * N_BLK)
    picks = jax.vmap(lambda single: jax.random.permutation(single, TILES * TILES)[:SLOTS])(many_keys)
    return picks.reshape(N_BLK, N_BLK, SLOTS).astype(jnp.int32)


def draw_tile_counts(key, part):
    key = jax.random.fold_in(key, 11)
    load_key, count_key, peak_key = jax.random.split(key, 3)
    device_load = jax.random.randint(load_key, (N_BLK, 1), max(1, SLOTS // 3), SLOTS + 1)
    lower_bound = jnp.maximum(device_load // 2, 1)
    counts = jax.random.randint(count_key, (N_BLK, N_BLK), lower_bound, device_load + 1)
    peak_spot = jax.random.randint(peak_key, (), 0, N_BLK * N_BLK)
    counts = counts.reshape(-1).at[peak_spot].set(SLOTS).reshape(N_BLK, N_BLK)
    return counts.astype(jnp.int32)


def shard_levels(rng, extent, pieces, low, largest):
    def one(dim, blocks):
        draws = jax.random.uniform(jax.random.fold_in(jax.random.fold_in(rng, 6), dim), (blocks,), jnp.float32, low / len(pieces), largest / len(pieces))
        return jnp.repeat(jnp.exp(draws), extent[dim] // blocks).reshape((-1,) + (1,) * (len(extent) - dim - 1))

    factor_of = one(*pieces[0])
    for cut in pieces[1:]:
        factor_of = factor_of * one(*cut)
    return factor_of


def gaussian(stream_key, dims, spread, most, cuts=(), held_as=jnp.bfloat16):
    result = jax.random.normal(stream_key, dims, jnp.float32) * spread
    if len(cuts) > 0:
        result = shard_levels(stream_key, dims, cuts, -0.22, 0.18) * result
    return jnp.clip(result, min=-most, max=most).astype(held_as)


def setup_inputs(seed: int = 0) -> dict:
    splits = jax.random.split(jax.random.key(seed), 7)
    return {
        "features": gaussian(splits[0], (NODES, FEATURES), 1.0, 6.0, ((0, 32),)),
        "layer_weight": gaussian(splits[1], (FEATURES, FEATURES), FEATURES ** -0.5, 0.25),
        "adjacency_tiles": gaussian(splits[2], (N_BLK, N_BLK, SLOTS, TILE, TILE), (N_BLK * SLOTS * TILE // (2 * TILES)) ** -0.5, 0.125, ((0, 32), (1, 8))),
        "tile_slots": draw_tile_slots(jax.random.fold_in(splits[6], 71), 0),
        "tile_counts": draw_tile_counts(jax.random.fold_in(splits[6], 71), 0),
        "cotangent": gaussian(splits[5], (NODES, FEATURES), 1.0, 6.0, ((0, 32),)),
    }


def gelu_tanh(value):
    return jax.nn.gelu(value, approximate=True)

def reference(features, layer_weight, adjacency_tiles, tile_slots, tile_counts, cotangent):
    highest = lax.Precision.HIGHEST
    feat_blocks = features.astype(jnp.float32).reshape(N_BLK, TILES, TILE, FEATURES)
    row_tile = (tile_slots // TILES).astype(jnp.int32)
    col_tile = (tile_slots % TILES).astype(jnp.int32)
    valid = (jnp.arange(SLOTS, dtype=jnp.int32)[None, None, :] < tile_counts[:, :, None]).astype(jnp.float32)
    offsets = jnp.arange(N_BLK, dtype=jnp.int32) - STEPS // 2
    tile_range = jnp.arange(TILES, dtype=jnp.int32)

    def forward_block(block_index):
        columns = (block_index + offsets) % N_BLK
        picked = feat_blocks[columns[:, None], col_tile[block_index]]
        weights = adjacency_tiles[block_index].astype(jnp.float32) * valid[block_index][:, :, None, None]
        product = jnp.einsum('jkpq,jkqf->jkpf', weights, picked, precision=highest)
        onehot = (row_tile[block_index][:, :, None] == tile_range).astype(jnp.float32)
        return jnp.einsum('jkt,jkpf->tpf', onehot, product, precision=highest)
    aggregated_full = lax.map(forward_block, jnp.arange(N_BLK, dtype=jnp.int32))
    aggregated = aggregated_full.reshape(NODES, FEATURES).astype(jnp.bfloat16)
    pre = jnp.dot(aggregated, layer_weight, preferred_element_type=jnp.float32)
    activated, pullback = jax.vjp(gelu_tanh, pre)
    delta = pullback(cotangent.astype(jnp.float32))[0].astype(jnp.bfloat16)
    grad_weight = jnp.dot(aggregated.T, delta, preferred_element_type=jnp.float32) * (1.0 / math.sqrt(NODES))
    back = jnp.dot(delta, layer_weight.T, preferred_element_type=jnp.float32).astype(jnp.bfloat16)
    back_blocks = back.astype(jnp.float32).reshape(N_BLK, TILES, TILE, FEATURES)

    def backward_block(carry, block_index):
        columns = (block_index + offsets) % N_BLK
        gathered = back_blocks[block_index][row_tile[block_index]]
        weights = adjacency_tiles[block_index].astype(jnp.float32) * valid[block_index][:, :, None, None]
        contrib = jnp.einsum('jkpq,jkpf->jkqf', weights, gathered, precision=highest)
        onehot = (col_tile[block_index][:, :, None] == tile_range).astype(jnp.float32)
        landed = jnp.einsum('jkt,jkqf->jtqf', onehot, contrib, precision=highest)
        return (carry.at[columns].add(landed), None)
    initial = jnp.zeros((N_BLK, TILES, TILE, FEATURES), jnp.float32)
    grad_full, _ = lax.scan(backward_block, initial, jnp.arange(N_BLK, dtype=jnp.int32))
    grad_input = grad_full.reshape(NODES, FEATURES).astype(jnp.bfloat16)
    return (activated.astype(jnp.bfloat16), grad_input, grad_weight)
```

```python
import math

import jax
import jax.numpy as jnp
from jax import lax
from jax.experimental import pallas as pl
from jax.experimental.pallas import tpu as pltpu
from jax.sharding import PartitionSpec as P

MESH = pl.DeviceIdType.MESH
F32, BF16 = jnp.float32, jnp.bfloat16
FEATURES = 512
TILE = 128
TILES = 8
SLOTS = 8
ROWS = 1024
GROUP = 256
GROUPS = ROWS // GROUP
K0 = math.sqrt(2.0 / math.pi)
K1 = 0.044715


def tile_rows(t):
    return pl.ds(pl.multiple_of(t * TILE, TILE), TILE)


def group_rows(g):
    return pl.ds(pl.multiple_of(g * GROUP, GROUP), GROUP)


def part_rows(p):
    return pl.ds(pl.multiple_of(p * 16, 16), 16)


def remote(src, dst, send, recv, blk, rep):
    return pltpu.make_async_remote_copy(
        src_ref=src, dst_ref=dst, send_sem=send, recv_sem=recv,
        device_id=(blk, rep), device_id_type=MESH,
    )


def landed(dst, sem):
    pltpu.make_async_copy(dst, dst, sem).wait()


def dot(a, b):
    return jnp.dot(a, b, preferred_element_type=F32)


def kernel(
    feat, w, tiles, inv, cot, act, gin, gw,
    wt, tl, tt, invv, invs, dense, denset, ring, blocks, acc, part, parts, agg, back,
    sib_out, sib_in, own_out, heap, hop_out, hop_in,
    gw_part, gw_send, gw_recv, gw_half, gw_quarter, gw_ring, gw_fin,
    t_s, t_r, i_s, i_r, i_l, z_s, z_r, f_s, f_r, s_s, s_r, p_s, p_r, a_s, a_r,
    b_s, b_r, o_s, o_r, h_s, h_r, g_s, g_r,
    wx_s, wx_r, wq_s, wq_r, wz_s, wz_r, wf_s, wf_r, wy_s, wy_r,
):
    b = lax.axis_index("blk")
    r = lax.axis_index("rep")
    z, q = b // 4, b % 4
    yh, core = q // 2, q % 2
    me = yh * 8 + r
    sib = b + 1 - 2 * core
    up = ((z + 1) % 8) * 4 + q
    down = ((z + 7) % 8) * 4 + q
    mine = tile_rows(r)

    def plane(y):
        return 4 * z + 2 * y + core

    barrier = pltpu.get_barrier_semaphore()
    for blk in (sib, up, down):
        pl.semaphore_signal(barrier, inc=1, device_id=(blk, r), device_id_type=MESH)

    @pl.loop(1, 16)
    def _(i):
        p = (me + i) % 16
        pl.semaphore_signal(barrier, inc=1, device_id=(plane(p // 8), p % 8), device_id_type=MESH)

    pl.semaphore_wait(barrier, 18)

    own = feat.at[mine]

    def spread(d):
        src = own if d == 0 else ring.at[d]
        dst = blocks.at[q, mine]
        for y in range(2):
            here = (yh == y) & (r == d)

            @pl.when(here)
            def _():
                pltpu.make_async_copy(src, dst, f_r.at[me]).start()

            @pl.when(jnp.logical_not(here))
            def _():
                remote(src, dst, f_s.at[y * 8 + d], f_r.at[me], plane(y), d).start()

    remote(own, ring.at[1], z_s.at[1], z_r.at[1], down, r).start()
    remote(own, ring.at[7], z_s.at[7], z_r.at[7], up, r).start()
    for m in range(4):
        off = q - 2 + m
        turn = jnp.where(off < 0, -1, jnp.where(off >= 4, 1, 0))
        slot = (off + 4) % 4
        to = (r + turn + 8) % 8

        @pl.when(turn == 0)
        def _():
            pltpu.make_async_copy(tiles.at[m], tl.at[slot, pl.ds(0, SLOTS)], t_r.at[slot]).start()
            pltpu.make_async_copy(inv.at[m], invv.at[slot], i_r.at[slot]).start()

        @pl.when(turn != 0)
        def _():
            remote(tiles.at[m], tl.at[slot, pl.ds(0, SLOTS)], t_s.at[m], t_r.at[slot], b, to).start()
            remote(inv.at[m], invv.at[slot], i_s.at[m], i_r.at[slot], b, to).start()

    spread(0)
    for k in range(1, 3):
        landed(ring.at[k], z_r.at[k])
        remote(ring.at[k], ring.at[k + 1], z_s.at[k + 1], z_r.at[k + 1], down, r).start()
        landed(ring.at[8 - k], z_r.at[8 - k])
        remote(ring.at[8 - k], ring.at[7 - k], z_s.at[7 - k], z_r.at[7 - k], up, r).start()
        spread(k)
        spread(8 - k)
    low, high = pl.ds(0, TILE // 2), pl.ds(TILE // 2, TILE // 2)
    landed(ring.at[3], z_r.at[3])
    remote(ring.at[3, low], ring.at[4, low], z_s.at[4], z_r.at[4], down, r).start()
    landed(ring.at[5], z_r.at[5])
    remote(ring.at[5, high], ring.at[4, high], z_s.at[0], z_r.at[0], up, r).start()
    spread(3)
    spread(5)
    landed(ring.at[4, low], z_r.at[4])
    landed(ring.at[4, high], z_r.at[0])
    spread(4)

    wt[...] = w[...].T
    for s in range(4):
        landed(tl.at[s, pl.ds(0, SLOTS)], t_r.at[s])
        landed(invv.at[s], i_r.at[s])
    move = pltpu.make_async_copy(invv, invs, i_l.at[0])
    move.start()
    zero = jnp.zeros((TILE, TILE), BF16)
    for s in range(4):
        tl[s, SLOTS] = zero
        tt[s, SLOTS] = zero

    @pl.loop(0, 4 * SLOTS)
    def _(i):
        tt[i // SLOTS, i % SLOTS] = tl[i // SLOTS, i % SLOTS].T

    move.wait()

    @pl.loop(0, 4 * TILES)
    def _(i):
        s, t = i // TILES, i % TILES
        for c in range(TILES):
            dense[s, tile_rows(t), c * TILE:(c + 1) * TILE] = tl[s, invs[s, 0, t * TILES + c]]
            denset[s, tile_rows(t), c * TILE:(c + 1) * TILE] = tt[s, invs[s, 0, c * TILES + t]]

    def pass_on(y):
        @pl.loop(0, 8)
        def _(s):
            piece = blocks.at[2 * y + core, tile_rows(s)]
            landed(piece, f_r.at[y * 8 + s])
            remote(piece, piece, s_s.at[y * 8 + s], s_r.at[y * 8 + s], sib, r).start()

    def take(y):
        @pl.loop(0, 8)
        def _(s):
            landed(blocks.at[2 * y + 1 - core, tile_rows(s)], s_r.at[y * 8 + s])

    def add_block(slot, first):
        @pl.loop(0, GROUPS)
        def _(g):
            rows = group_rows(g)
            value = dot(dense[slot, rows, :], blocks[slot])
            acc[rows] = value if first else acc[rows] + value

    pass_on(0)
    pass_on(1)
    add_block(core, True)
    add_block(2 + core, False)
    take(0)
    add_block(1 - core, False)
    take(1)

    @pl.loop(0, GROUPS)
    def _(i):
        g = (r // 2 + 1 + i) % GROUPS
        rows = group_rows(g)
        part[rows] = (acc[rows] + dot(dense[3 - core, rows, :], blocks[3 - core])).astype(BF16)
        for h in range(2):
            t = 2 * g + h

            @pl.when(t != r)
            def _():
                remote(part.at[tile_rows(t)], parts.at[r], p_s.at[t], p_r.at[r], b, t).start()

    acc[0:TILE] = part[mine].astype(F32)

    @pl.loop(1, 8)
    def _(i):
        p = (r + 8 - i) % 8
        landed(parts.at[p], p_r.at[p])
        acc[0:TILE] += parts[p].astype(F32)

    agg[mine] = acc[0:TILE].astype(BF16)

    @pl.loop(1, 8)
    def _(i):
        t = (r + i) % 8
        remote(agg.at[mine], agg.at[mine], a_s.at[t], a_r.at[r], b, t).start()

    def chunk(c):
        rows = tile_rows(c)
        pre = dot(agg[rows], w[...])
        square = pre * pre
        t = jnp.tanh(K0 * (pre + K1 * square * pre))
        half = 0.5 * (1.0 + t)
        act[rows] = (pre * half).astype(BF16)
        slope = half + 0.5 * pre * (1.0 - t * t) * (K0 * (1.0 + 3.0 * K1 * square))
        delta = (cot[rows].astype(F32) * slope).astype(BF16)
        back[rows] = dot(delta, wt[...]).astype(BF16)
        return delta

    delta = chunk(r)
    gw_part[...] = lax.dot_general(
        agg[mine], delta, (((0,), (0,)), ((), ())), preferred_element_type=F32
    )
    gw_send[...] = gw_part[group_rows(1 - core)].astype(BF16)
    remote(gw_send, gw_recv, wx_s.at[0], wx_r.at[0], sib, r).start()

    @pl.loop(1, 8)
    def _(i):
        c = (r + 8 - i) % 8
        landed(agg.at[tile_rows(c)], a_r.at[c])
        chunk(c)

    for y in range(2):
        @pl.loop(0, GROUPS)
        def _(g):
            rows = group_rows(g)
            sib_out[y, rows] = dot(denset[2 * y + 1 - core, rows, :], back[...]).astype(BF16)
            remote(
                sib_out.at[y, rows], sib_in.at[y, rows], b_s.at[y * 4 + g], b_r.at[y * 4 + g], sib, r
            ).start()

    landed(gw_recv, wx_r.at[0])
    gw_half[...] = (gw_part[group_rows(core)] + gw_recv[...].astype(F32)).astype(BF16)

    @pl.loop(1, 16)
    def _(i):
        p = (me + i) % 16
        remote(
            gw_half.at[part_rows(p)], gw_quarter.at[part_rows(me)], wq_s.at[p], wq_r.at[me],
            plane(p // 8), p % 8,
        ).start()

    for y in range(2):
        @pl.loop(0, GROUPS)
        def _(i):
            g = (r // 2 + 1 + i) % GROUPS
            rows = group_rows(g)
            value = dot(denset[2 * y + core, rows, :], back[...])
            landed(sib_in.at[y, rows], b_r.at[y * 4 + g])
            own_out[y, rows] = (value + sib_in[y, rows].astype(F32)).astype(BF16)
            for h in range(2):
                t = 2 * g + h
                src, dst = own_out.at[y, tile_rows(t)], heap.at[me]
                here = (yh == y) & (r == t)

                @pl.when(here)
                def _():
                    pltpu.make_async_copy(src, dst, o_r.at[me]).start()

                @pl.when(jnp.logical_not(here))
                def _():
                    remote(src, dst, o_s.at[y * 8 + t], o_r.at[me], plane(y), t).start()

    gw_ring[0] = gw_half[part_rows(me)].astype(F32)

    @pl.loop(1, 16)
    def _(i):
        p = (me + i) % 16
        landed(gw_quarter.at[part_rows(p)], wq_r.at[p])
        gw_ring[0] += gw_quarter[part_rows(p)].astype(F32)

    for k in range(4):
        if k > 0:
            landed(gw_ring.at[k], wz_r.at[k])
        remote(gw_ring.at[k], gw_ring.at[k + 1], wz_s.at[k + 1], wz_r.at[k + 1], down, r).start()
        if k < 3:
            j = (8 - k) % 8
            if k > 0:
                landed(gw_ring.at[j], wz_r.at[j])
            remote(gw_ring.at[j], gw_ring.at[7 - k], wz_s.at[7 - k], wz_r.at[7 - k], up, r).start()
    landed(gw_ring.at[4], wz_r.at[4])
    landed(gw_ring.at[5], wz_r.at[5])
    total = gw_ring[(8 - z) % 8]
    for k in range(1, 8):
        total = total + gw_ring[(k + 8 - z) % 8]
    place = pl.ds(pl.multiple_of(core * 256 + me * 16, 16), 16)
    gw_fin[place] = (total * (1.0 / math.sqrt(32 * ROWS))).astype(BF16)

    @pl.loop(1, 16)
    def _(i):
        p = (me + i) % 16
        remote(
            gw_fin.at[place], gw_fin.at[place], wf_s.at[p], wf_r.at[me], plane(p // 8), p % 8
        ).start()

    def plane_sum(d):
        landed(heap.at[d], o_r.at[d])
        landed(heap.at[8 + d], o_r.at[8 + d])
        return heap[d].astype(F32) + heap[8 + d].astype(F32)

    hop_out[4] = plane_sum(4).astype(BF16)
    remote(hop_out.at[4, low], hop_in.at[3, low], h_s.at[3], h_r.at[3], up, r).start()
    remote(hop_out.at[4, high], hop_in.at[5, high], h_s.at[5], h_r.at[5], down, r).start()
    for k in (3, 2, 1):
        for d, here_rows, to, then in (
            (k, low, up, k - 1),
            (8 - k, high, down, 9 - k if k > 1 else 4),
        ):
            value = plane_sum(d)
            if k == 3:
                hop_out[d] = value.astype(BF16)
                landed(hop_in.at[d, here_rows], h_r.at[d])
                hop_out[d, here_rows] = (
                    heap[d, here_rows].astype(F32)
                    + heap[8 + d, here_rows].astype(F32)
                    + hop_in[d, here_rows].astype(F32)
                ).astype(BF16)
            else:
                landed(hop_in.at[d], h_r.at[d])
                hop_out[d] = (value + hop_in[d].astype(F32)).astype(BF16)
            remote(hop_out.at[d], hop_in.at[then], h_s.at[then], h_r.at[then], to, r).start()
    value = plane_sum(0)
    landed(hop_in.at[0], h_r.at[0])
    landed(hop_in.at[4], h_r.at[4])
    gin[mine] = (value + hop_in[0].astype(F32) + hop_in[4].astype(F32)).astype(BF16)

    @pl.loop(1, 8)
    def _(i):
        t = (r + i) % 8
        remote(gin.at[mine], gin.at[mine], g_s.at[t], g_r.at[r], b, t).start()

    @pl.loop(1, 16)
    def _(i):
        p = (me + i) % 16
        rows = pl.ds(pl.multiple_of(core * 256 + p * 16, 16), 16)
        landed(gw_fin.at[rows], wf_r.at[p])

    half = group_rows(core)
    remote(gw_fin.at[half], gw_fin.at[half], wy_s.at[0], wy_r.at[0], sib, r).start()
    landed(gw_fin.at[group_rows(1 - core)], wy_r.at[0])
    gw[...] = gw_fin[...].astype(F32)

    @pl.loop(1, 8)
    def _(i):
        c = (r + 8 - i) % 8
        landed(gin.at[tile_rows(c)], g_r.at[c])

    for m in range(4):
        off = q - 2 + m

        @pl.when((off < 0) | (off >= 4))
        def _():
            landed(tiles.at[m], t_s.at[m])
            landed(inv.at[m], i_s.at[m])

    for d in (1, 2, 3, 5, 6, 7):
        landed(ring.at[d], z_s.at[d])
    landed(ring.at[4, low], z_s.at[4])
    landed(ring.at[4, high], z_s.at[0])

    @pl.loop(0, 16)
    def _(p):
        landed(blocks.at[0, tile_rows(0)], s_s.at[p])

    @pl.loop(1, 16)
    def _(i):
        p = (me + i) % 16
        landed(blocks.at[0, tile_rows(0)], f_s.at[p])
        landed(heap.at[0], o_s.at[p])
        landed(gw_half.at[part_rows(0)], wq_s.at[p])
        landed(gw_fin.at[part_rows(0)], wf_s.at[p])

    @pl.loop(1, 8)
    def _(i):
        t = (r + i) % 8
        landed(parts.at[0], p_s.at[t])
        landed(agg.at[tile_rows(0)], a_s.at[t])
        landed(gin.at[tile_rows(0)], g_s.at[t])

    @pl.loop(0, 8)
    def _(i):
        landed(sib_out.at[0, group_rows(0)], b_s.at[i])

    landed(gw_send, wx_s.at[0])
    landed(gw_fin.at[half], wy_s.at[0])
    for d in range(1, 8):
        landed(gw_ring.at[d], wz_s.at[d])
    landed(hop_in.at[3, low], h_s.at[3])
    landed(hop_in.at[5, high], h_s.at[5])
    for d in (0, 1, 2, 4, 6, 7):
        landed(hop_in.at[d], h_s.at[d])


def per_device(features, layer_weight, adjacency_tiles, tile_slots, tile_counts, cotangent):
    slots, counts = tile_slots[0], tile_counts[0]
    place = jnp.arange(SLOTS, dtype=jnp.int32)
    live = place[None, :] < counts[:, None]
    hot = (slots[:, :, None] == jnp.arange(TILE, dtype=jnp.int32)) & live[:, :, None]
    index = jnp.sum(jnp.where(hot, place[None, :, None] - SLOTS, 0), axis=1) + SLOTS
    index = jnp.broadcast_to(index[:, None, :], (4, 8, TILE)).astype(jnp.int32)
    vm = pl.BlockSpec(memory_space=pltpu.VMEM)
    dma = pltpu.SemaphoreType.DMA
    scratch = [
        pltpu.VMEM((FEATURES, FEATURES), BF16),
        pltpu.VMEM((4, SLOTS + 1, TILE, TILE), BF16),
        pltpu.VMEM((4, SLOTS + 1, TILE, TILE), BF16),
        pltpu.VMEM((4, 8, TILE), jnp.int32),
        pltpu.SMEM((4, 8, TILE), jnp.int32),
        pltpu.VMEM((4, ROWS, ROWS), BF16),
        pltpu.VMEM((4, ROWS, ROWS), BF16),
        pltpu.VMEM((8, TILE, FEATURES), BF16),
        pltpu.VMEM((4, ROWS, FEATURES), BF16),
        pltpu.VMEM((ROWS, FEATURES), F32),
        pltpu.VMEM((ROWS, FEATURES), BF16),
        pltpu.VMEM((8, TILE, FEATURES), BF16),
        pltpu.VMEM((ROWS, FEATURES), BF16),
        pltpu.VMEM((ROWS, FEATURES), BF16),
        pltpu.VMEM((2, ROWS, FEATURES), BF16),
        pltpu.VMEM((2, ROWS, FEATURES), BF16),
        pltpu.VMEM((2, ROWS, FEATURES), BF16),
        pltpu.VMEM((16, TILE, FEATURES), BF16),
        pltpu.VMEM((8, TILE, FEATURES), BF16),
        pltpu.VMEM((8, TILE, FEATURES), BF16),
        pltpu.VMEM((FEATURES, FEATURES), F32),
        pltpu.VMEM((256, FEATURES), BF16),
        pltpu.VMEM((256, FEATURES), BF16),
        pltpu.VMEM((256, FEATURES), BF16),
        pltpu.VMEM((256, FEATURES), BF16),
        pltpu.VMEM((8, 16, FEATURES), F32),
        pltpu.VMEM((FEATURES, FEATURES), BF16),
    ]
    sems = [4, 4, 4, 4, 1, 8, 8, 16, 16, 16, 16, 8, 8, 8, 8, 8, 8, 16, 16, 8, 8, 8, 8,
            1, 1, 16, 16, 8, 8, 16, 16, 1, 1]
    return pl.pallas_call(
        kernel,
        out_shape=(
            jax.ShapeDtypeStruct((ROWS, FEATURES), BF16),
            jax.ShapeDtypeStruct((ROWS, FEATURES), BF16),
            jax.ShapeDtypeStruct((FEATURES, FEATURES), F32),
        ),
        in_specs=[vm] * 5,
        out_specs=(vm, vm, vm),
        scratch_shapes=scratch + [dma((n,)) for n in sems],
        compiler_params=pltpu.CompilerParams(
            collective_id=0, has_side_effects=True, vmem_limit_bytes=58 * 1024 * 1024
        ),
        cost_estimate=pl.CostEstimate(
            flops=10 * 2 * ROWS * ROWS * FEATURES, bytes_accessed=8 << 20, transcendentals=ROWS * FEATURES
        ),
    )(features, layer_weight, adjacency_tiles[0], index, cotangent)


def solution(mesh):
    return jax.shard_map(
        per_device,
        mesh=mesh,
        in_specs=(
            P("blk", None),
            P(),
            P("blk", "rep", None, None, None),
            P("blk", "rep", None),
            P("blk", "rep"),
            P("blk", None),
        ),
        out_specs=(P("blk", None), P("blk", None), P()),
        check_vma=False,
    )
```

```python
import math

import jax
import jax.numpy as jnp
from jax import lax
from jax.experimental import pallas as pl
from jax.experimental.pallas import tpu as pltpu
from jax.sharding import PartitionSpec as P

MESH = pl.DeviceIdType.MESH
F32, BF16 = jnp.float32, jnp.bfloat16
FEATURES = 512
TILE = 128
TILES = 8
SLOTS = 8
ROWS = 1024
GROUP = 256
GROUPS = ROWS // GROUP
HALVES = 2
WIDTH = FEATURES // HALVES
K0 = math.sqrt(2.0 / math.pi)
K1 = 0.044715


def tile_rows(t):
    return pl.ds(pl.multiple_of(t * TILE, TILE), TILE)


def group_rows(g):
    return pl.ds(pl.multiple_of(g * GROUP, GROUP), GROUP)


def part_rows(p):
    return pl.ds(pl.multiple_of(p * 16, 16), 16)


def half_columns(h):
    return pl.ds(h * WIDTH, WIDTH)


def remote(src, dst, send, recv, blk, rep):
    return pltpu.make_async_remote_copy(
        src_ref=src, dst_ref=dst, send_sem=send, recv_sem=recv,
        device_id=(blk, rep), device_id_type=MESH,
    )


def landed(dst, sem):
    pltpu.make_async_copy(dst, dst, sem).wait()


def dot(a, b):
    return jnp.dot(a, b, preferred_element_type=F32)


def kernel(
    feat, w_in, tiles, inv, cot_in, act_out, gin, gw,
    w, wt, cot, act, tl, tt, invv, invs, dense, denset, ring, blocks, acc, part, parts, agg, back,
    sib_out, sib_in, own_out, heap, total, hop_out, hop_in, grad,
    gw_part, gw_send, gw_recv, gw_half, gw_quarter, gw_ring, gw_fin,
    in_s, out_s,
    t_s, t_r, i_s, i_r, i_l, z_s, z_r, f_s, f_r, s_s, s_r, p_s, p_r, a_s, a_r,
    b_s, b_r, o_s, o_r, h_s, h_r, g_s, g_r,
    wx_s, wx_r, wq_s, wq_r, wz_s, wz_r, wf_s, wf_r, wy_s, wy_r,
):
    b = lax.axis_index("blk")
    r = lax.axis_index("rep")
    z, q = b // 4, b % 4
    yh, core = q // 2, q % 2
    me = yh * 8 + r
    sib = b + 1 - 2 * core
    up = ((z + 1) % 8) * 4 + q
    down = ((z + 7) % 8) * 4 + q
    mine = tile_rows(r)
    low, high = pl.ds(0, TILE // 2), pl.ds(TILE // 2, TILE // 2)

    def plane(y):
        return 4 * z + 2 * y + core

    def along(d):
        return ((z + d) % 8) * 4 + q

    barrier = pltpu.get_barrier_semaphore()
    pl.semaphore_signal(barrier, inc=1, device_id=(sib, r), device_id_type=MESH)

    @pl.loop(1, 8)
    def _(d):
        pl.semaphore_signal(barrier, inc=1, device_id=(along(d), r), device_id_type=MESH)

    @pl.loop(1, 16)
    def _(i):
        p = (me + i) % 16
        pl.semaphore_signal(barrier, inc=1, device_id=(plane(p // 8), p % 8), device_id_type=MESH)

    take_w = pltpu.make_async_copy(w_in, w, in_s.at[0])
    take_w.start()
    take_cot = pltpu.make_async_copy(cot_in, cot, in_s.at[1])
    take_cot.start()
    pl.semaphore_wait(barrier, 23)

    sent = []

    def later(first, count, index, what, sem):
        def wait():
            @pl.loop(first, count)
            def _(i):
                landed(what, sem.at[index(i)])

        sent.append(wait)

    def peer(i):
        return (me + i) % 16

    def fellow(i):
        return (r + i) % 8

    def same(i):
        return i

    def own(h):
        return feat.at[mine, half_columns(h)]

    def spread(h, d):
        src = own(h) if d == 0 else ring.at[h, d]
        dst = blocks.at[h, q, mine]
        for y in range(2):
            here = (yh == y) & (r == d)

            @pl.when(here)
            def _():
                pltpu.make_async_copy(src, dst, f_r.at[h, me]).start()

            @pl.when(jnp.logical_not(here))
            def _():
                remote(src, dst, f_s.at[h, y * 8 + d], f_r.at[h, me], plane(y), d).start()

    for h in range(HALVES):
        remote(own(h), ring.at[h, 1], z_s.at[h, 1], z_r.at[h, 1], down, r).start()
        remote(own(h), ring.at[h, 7], z_s.at[h, 7], z_r.at[h, 7], up, r).start()
    for m in range(4):
        off = q - 2 + m
        turn = jnp.where(off < 0, -1, jnp.where(off >= 4, 1, 0))
        slot = (off + 4) % 4
        to = (r + turn + 8) % 8

        @pl.when(turn == 0)
        def _():
            pltpu.make_async_copy(tiles.at[m], tl.at[slot, pl.ds(0, SLOTS)], t_r.at[slot]).start()
            pltpu.make_async_copy(inv.at[m], invv.at[slot], i_r.at[slot]).start()

        @pl.when(turn != 0)
        def _():
            remote(tiles.at[m], tl.at[slot, pl.ds(0, SLOTS)], t_s.at[m], t_r.at[slot], b, to).start()
            remote(inv.at[m], invv.at[slot], i_s.at[m], i_r.at[slot], b, to).start()

    def forward_ring(h, k):
        landed(ring.at[h, k], z_r.at[h, k])
        landed(ring.at[h, 8 - k], z_r.at[h, 8 - k])
        if k < 3:
            remote(ring.at[h, k], ring.at[h, k + 1], z_s.at[h, k + 1], z_r.at[h, k + 1], down, r).start()
            remote(ring.at[h, 8 - k], ring.at[h, 7 - k], z_s.at[h, 7 - k], z_r.at[h, 7 - k], up, r).start()
        else:
            remote(ring.at[h, 3, low], ring.at[h, 4, low], z_s.at[h, 4], z_r.at[h, 4], down, r).start()
            remote(ring.at[h, 5, high], ring.at[h, 4, high], z_s.at[h, 0], z_r.at[h, 0], up, r).start()

    def last_of_ring(h):
        landed(ring.at[h, 4, low], z_r.at[h, 4])
        landed(ring.at[h, 4, high], z_r.at[h, 0])

    spread(0, 0)
    for k in range(1, 4):
        forward_ring(0, k)
        spread(0, k)
        spread(0, 8 - k)
        forward_ring(1, k)
        if k == 2:
            spread(1, 0)
        if k == 3:
            spread(1, 1)
            spread(1, 7)
    last_of_ring(0)
    spread(0, 4)
    for d in (2, 6, 3, 5):
        spread(1, d)
    last_of_ring(1)
    spread(1, 4)
    for h in range(HALVES):
        later(1, 16, peer, blocks.at[0, 0, tile_rows(0)], f_s.at[h])
        later(1, 4, same, ring.at[0, 0], z_s.at[h])
        later(5, 8, same, ring.at[0, 0], z_s.at[h])
        later(0, 1, lambda i: 4, ring.at[0, 4, low], z_s.at[h])
        later(0, 1, lambda i: 0, ring.at[0, 4, low], z_s.at[h])

    def lists_sent():
        for m in range(4):
            off = q - 2 + m

            @pl.when((off < 0) | (off >= 4))
            def _():
                landed(tiles.at[m], t_s.at[m])
                landed(inv.at[m], i_s.at[m])

    sent.append(lists_sent)
    take_w.wait()
    wt[...] = w[...].T
    for s in range(4):
        landed(tl.at[s, pl.ds(0, SLOTS)], t_r.at[s])
        landed(invv.at[s], i_r.at[s])
    move = pltpu.make_async_copy(invv, invs, i_l.at[0])
    move.start()
    zero = jnp.zeros((TILE, TILE), BF16)
    for s in range(4):
        tl[s, SLOTS] = zero
        tt[s, SLOTS] = zero

    @pl.loop(0, 4 * SLOTS)
    def _(i):
        tt[i // SLOTS, i % SLOTS] = tl[i // SLOTS, i % SLOTS].T

    move.wait()

    @pl.loop(0, 4 * TILES)
    def _(i):
        s, t = i // TILES, i % TILES
        for c in range(TILES):
            dense[s, tile_rows(t), c * TILE:(c + 1) * TILE] = tl[s, invs[s, 0, t * TILES + c]]
            denset[s, tile_rows(t), c * TILE:(c + 1) * TILE] = tt[s, invs[s, 0, c * TILES + t]]

    take_cot.wait()

    def pass_on(h):
        @pl.loop(0, 16)
        def _(i):
            piece = blocks.at[h, 2 * (i // 8) + core, tile_rows(i % 8)]
            landed(piece, f_r.at[h, i])
            remote(piece, piece, s_s.at[h, i], s_r.at[h, i], sib, r).start()

        later(0, 16, same, blocks.at[0, 0, tile_rows(0)], s_s.at[h])

    def own_blocks(h):
        @pl.loop(0, GROUPS)
        def _(g):
            rows = group_rows(g)
            acc[h, rows] = dot(dense[core, rows, :], blocks[h, core]) + dot(
                dense[2 + core, rows, :], blocks[h, 2 + core]
            )

    def sibling_blocks(h):
        @pl.loop(0, 16)
        def _(i):
            landed(blocks.at[h, 2 * (i // 8) + 1 - core, tile_rows(i % 8)], s_r.at[h, i])

        @pl.loop(0, GROUPS)
        def _(i):
            g = (r // 2 + 1 + i) % GROUPS
            rows = group_rows(g)
            value = dot(dense[1 - core, rows, :], blocks[h, 1 - core]) + dot(
                dense[3 - core, rows, :], blocks[h, 3 - core]
            )
            part[h, rows] = (acc[h, rows] + value).astype(BF16)
            for j in range(2):
                t = 2 * g + j

                @pl.when(t != r)
                def _():
                    remote(part.at[h, tile_rows(t)], parts.at[h, r], p_s.at[h, t], p_r.at[h, r], b, t).start()

        later(1, 8, fellow, parts.at[0, 0], p_s.at[h])

    def add_parts(h):
        acc[h, 0:TILE] = part[h, mine].astype(F32)

        @pl.loop(1, 8)
        def _(i):
            p = (r + 8 - i) % 8
            landed(parts.at[h, p], p_r.at[h, p])
            acc[h, 0:TILE] += parts[h, p].astype(F32)

        agg[h, mine] = acc[h, 0:TILE].astype(BF16)

    def share(h):
        @pl.loop(1, 8)
        def _(i):
            t = (r + i) % 8
            remote(agg.at[h, mine], agg.at[h, mine], a_s.at[h, t], a_r.at[h, r], b, t).start()

        later(1, 8, fellow, agg.at[0, tile_rows(0)], a_s.at[h])

    pass_on(0)
    own_blocks(0)
    sibling_blocks(0)
    pass_on(1)
    own_blocks(1)
    add_parts(0)
    share(0)
    sibling_blocks(1)
    add_parts(1)
    share(1)

    def chunk(c):
        rows = tile_rows(c)
        pre = dot(agg[0, rows], w[0:WIDTH]) + dot(agg[1, rows], w[WIDTH:])
        square = pre * pre
        t = jnp.tanh(K0 * (pre + K1 * square * pre))
        half = 0.5 * (1.0 + t)
        act[rows] = (pre * half).astype(BF16)
        pltpu.make_async_copy(act.at[rows], act_out.at[rows], out_s.at[c]).start()
        slope = half + 0.5 * pre * (1.0 - t * t) * (K0 * (1.0 + 3.0 * K1 * square))
        delta = (cot[rows].astype(F32) * slope).astype(BF16)
        value = dot(delta, wt[...]).astype(BF16)
        for h in range(HALVES):
            back[h, rows] = value[:, h * WIDTH:(h + 1) * WIDTH]
        return delta

    delta = chunk(r)
    for h in range(HALVES):
        gw_part[h * WIDTH:(h + 1) * WIDTH] = lax.dot_general(
            agg[h, mine], delta, (((0,), (0,)), ((), ())), preferred_element_type=F32
        )
    gw_send[...] = gw_part[group_rows(1 - core)].astype(BF16)
    remote(gw_send, gw_recv, wx_s.at[0], wx_r.at[0], sib, r).start()
    later(0, 1, same, gw_send, wx_s)

    @pl.loop(1, 8)
    def _(i):
        c = (r + 8 - i) % 8
        landed(agg.at[0, tile_rows(c)], a_r.at[0, c])
        landed(agg.at[1, tile_rows(c)], a_r.at[1, c])
        chunk(c)

    landed(gw_recv, wx_r.at[0])
    gw_half[...] = (gw_part[group_rows(core)] + gw_recv[...].astype(F32)).astype(BF16)

    @pl.loop(1, 16)
    def _(i):
        p = (me + i) % 16
        remote(
            gw_half.at[part_rows(p)], gw_quarter.at[part_rows(me)], wq_s.at[p], wq_r.at[me],
            plane(p // 8), p % 8,
        ).start()

    later(1, 16, peer, gw_half.at[part_rows(0)], wq_s)
    for h in range(HALVES):
        @pl.loop(0, 2 * GROUPS)
        def _(i):
            y, g = i // GROUPS, i % GROUPS
            rows = group_rows(g)
            sib_out[h, y, rows] = dot(denset[2 * y + 1 - core, rows, :], back[h]).astype(BF16)
            remote(
                sib_out.at[h, y, rows], sib_in.at[h, y, rows], b_s.at[h, i], b_r.at[h, i], sib, r
            ).start()

        later(0, 8, same, sib_out.at[0, 0, group_rows(0)], b_s.at[h])

    def own_grads(h):
        @pl.loop(0, 2 * GROUPS)
        def _(i):
            y, g = i % 2, (r // 2 + 1 + i // 2) % GROUPS
            rows = group_rows(g)
            value = dot(denset[2 * y + core, rows, :], back[h])
            landed(sib_in.at[h, y, rows], b_r.at[h, y * GROUPS + g])
            own_out[h, y, rows] = (value + sib_in[h, y, rows].astype(F32)).astype(BF16)
            for j in range(2):
                t = 2 * g + j
                src, dst = own_out.at[h, y, tile_rows(t)], heap.at[h, me]
                here = (yh == y) & (r == t)

                @pl.when(here)
                def _():
                    pltpu.make_async_copy(src, dst, o_r.at[h, me]).start()

                @pl.when(jnp.logical_not(here))
                def _():
                    remote(src, dst, o_s.at[h, y * 8 + t], o_r.at[h, me], plane(y), t).start()

        later(1, 16, peer, heap.at[0, 0], o_s.at[h])

    own_grads(0)
    own_grads(1)
    gw_ring[0] = gw_half[part_rows(me)].astype(F32)

    @pl.loop(1, 16)
    def _(i):
        p = (me + i) % 16
        landed(gw_quarter.at[part_rows(p)], wq_r.at[p])
        gw_ring[0] += gw_quarter[part_rows(p)].astype(F32)

    @pl.loop(1, 8)
    def _(d):
        remote(gw_ring.at[0], gw_ring.at[d], wz_s.at[d], wz_r.at[d], along(d), r).start()

    later(1, 8, same, gw_ring.at[0], wz_s)

    def send_along(h):
        @pl.loop(0, 8)
        def _(i):
            d = 2 * ((r // 2 + 3 - i // 2) % 4) + i % 2
            landed(heap.at[h, d], o_r.at[h, d])
            landed(heap.at[h, 8 + d], o_r.at[h, 8 + d])
            value = heap[h, d].astype(F32) + heap[h, 8 + d].astype(F32)

            @pl.when(d == 0)
            def _():
                total[h] = value

            @pl.when(d != 0)
            def _():
                hop_out[h, d] = value.astype(BF16)
                remote(hop_out.at[h, d], hop_in.at[h, d], h_s.at[h, d], h_r.at[h, d], along(d), r).start()

        later(1, 8, same, hop_out.at[0, 0], h_s.at[h])

    def finish(h):
        @pl.loop(1, 8)
        def _(d):
            landed(hop_in.at[h, d], h_r.at[h, d])
            total[h] += hop_in[h, d].astype(F32)

        place = grad.at[h, mine]
        grad[h, mine] = total[h].astype(BF16)

        @pl.loop(1, 8)
        def _(i):
            t = (r + i) % 8
            remote(place, place, g_s.at[h, t], g_r.at[h, r], b, t).start()

        later(1, 8, fellow, place, g_s.at[h])

    send_along(0)
    @pl.loop(1, 8)
    def _(d):
        landed(gw_ring.at[d], wz_r.at[d])

    whole = gw_ring[z]
    for k in range(1, 8):
        whole = whole + gw_ring[(z + 8 - k) % 8]
    place = pl.ds(pl.multiple_of(core * 256 + me * 16, 16), 16)
    gw_fin[place] = (whole * (1.0 / math.sqrt(32 * ROWS))).astype(BF16)

    @pl.loop(1, 16)
    def _(i):
        p = (me + i) % 16
        remote(
            gw_fin.at[place], gw_fin.at[place], wf_s.at[p], wf_r.at[me], plane(p // 8), p % 8
        ).start()

    later(1, 16, peer, gw_fin.at[part_rows(0)], wf_s)

    finish(0)
    send_along(1)
    finish(1)

    @pl.loop(1, 16)
    def _(i):
        p = (me + i) % 16
        rows = pl.ds(pl.multiple_of(core * 256 + p * 16, 16), 16)
        landed(gw_fin.at[rows], wf_r.at[p])

    @pl.loop(0, 8)
    def _(i):
        landed(act.at[tile_rows(i)], out_s.at[i])

    half = group_rows(core)
    remote(gw_fin.at[half], gw_fin.at[half], wy_s.at[0], wy_r.at[0], sib, r).start()
    later(0, 1, same, gw_fin.at[half], wy_s)
    landed(gw_fin.at[group_rows(1 - core)], wy_r.at[0])
    give_gw = pltpu.make_async_copy(gw_fin, gw, in_s.at[0])
    give_gw.start()

    for h in range(HALVES):
        @pl.loop(1, 8)
        def _(i):
            c = (r + 8 - i) % 8
            landed(grad.at[h, tile_rows(c)], g_r.at[h, c])

        pltpu.make_async_copy(grad.at[h], gin.at[:, half_columns(h)], out_s.at[h]).start()

    for wait in sent:
        wait()
    give_gw.wait()
    for h in range(HALVES):
        landed(grad.at[h], out_s.at[h])


def per_device(features, layer_weight, adjacency_tiles, tile_slots, tile_counts, cotangent):
    slots, counts = tile_slots[0], tile_counts[0]
    place = jnp.arange(SLOTS, dtype=jnp.int32)
    live = place[None, :] < counts[:, None]
    hot = (slots[:, :, None] == jnp.arange(TILE, dtype=jnp.int32)) & live[:, :, None]
    index = jnp.sum(jnp.where(hot, place[None, :, None] - SLOTS, 0), axis=1) + SLOTS
    index = jnp.broadcast_to(index[:, None, :], (4, 8, TILE)).astype(jnp.int32)
    hbm = pl.BlockSpec(memory_space=pl.ANY)
    dma = pltpu.SemaphoreType.DMA
    half = (HALVES, ROWS, WIDTH)
    slices = (HALVES, 8, TILE, WIDTH)
    scratch = [
        pltpu.VMEM((FEATURES, FEATURES), BF16),
        pltpu.VMEM((FEATURES, FEATURES), BF16),
        pltpu.VMEM((ROWS, FEATURES), BF16),
        pltpu.VMEM((ROWS, FEATURES), BF16),
        pltpu.VMEM((4, SLOTS + 1, TILE, TILE), BF16),
        pltpu.VMEM((4, SLOTS + 1, TILE, TILE), BF16),
        pltpu.VMEM((4, 8, TILE), jnp.int32),
        pltpu.SMEM((4, 8, TILE), jnp.int32),
        pltpu.VMEM((4, ROWS, ROWS), BF16),
        pltpu.VMEM((4, ROWS, ROWS), BF16),
        pltpu.VMEM(slices, BF16),
        pltpu.VMEM((HALVES, 4, ROWS, WIDTH), BF16),
        pltpu.VMEM(half, F32),
        pltpu.VMEM(half, BF16),
        pltpu.VMEM(slices, BF16),
        pltpu.VMEM(half, BF16),
        pltpu.VMEM(half, BF16),
        pltpu.VMEM((HALVES, 2, ROWS, WIDTH), BF16),
        pltpu.VMEM((HALVES, 2, ROWS, WIDTH), BF16),
        pltpu.VMEM((HALVES, 2, ROWS, WIDTH), BF16),
        pltpu.VMEM((HALVES, 16, TILE, WIDTH), BF16),
        pltpu.VMEM((HALVES, TILE, WIDTH), F32),
        pltpu.VMEM(slices, BF16),
        pltpu.VMEM(slices, BF16),
        pltpu.VMEM(half, BF16),
        pltpu.VMEM((FEATURES, FEATURES), F32),
        pltpu.VMEM((256, FEATURES), BF16),
        pltpu.VMEM((256, FEATURES), BF16),
        pltpu.VMEM((256, FEATURES), BF16),
        pltpu.VMEM((256, FEATURES), BF16),
        pltpu.VMEM((8, 16, FEATURES), F32),
        pltpu.VMEM((FEATURES, FEATURES), BF16),
    ]
    two = HALVES
    sems = [
        (2,), (8,),
        (4,), (4,), (4,), (4,), (1,), (two, 8), (two, 8), (two, 16), (two, 16), (two, 16), (two, 16),
        (two, 8), (two, 8), (two, 8), (two, 8),
        (two, 8), (two, 8), (two, 16), (two, 16), (two, 8), (two, 8), (two, 8), (two, 8),
        (1,), (1,), (16,), (16,), (8,), (8,), (16,), (16,), (1,), (1,),
    ]
    activated, grad_input, grad_weight = pl.pallas_call(
        kernel,
        out_shape=(
            jax.ShapeDtypeStruct((ROWS, FEATURES), BF16),
            jax.ShapeDtypeStruct((ROWS, FEATURES), BF16),
            jax.ShapeDtypeStruct((FEATURES, FEATURES), BF16),
        ),
        in_specs=[hbm] * 5,
        out_specs=(hbm, hbm, hbm),
        scratch_shapes=scratch + [dma(n) for n in sems],
        compiler_params=pltpu.CompilerParams(
            collective_id=0, has_side_effects=True, vmem_limit_bytes=58 * 1024 * 1024
        ),
        cost_estimate=pl.CostEstimate(
            flops=10 * 2 * ROWS * ROWS * FEATURES, bytes_accessed=8 << 20, transcendentals=ROWS * FEATURES
        ),
    )(features, layer_weight, adjacency_tiles[0], index, cotangent)
    return activated, grad_input, grad_weight.astype(F32)


def solution(mesh):
    return jax.shard_map(
        per_device,
        mesh=mesh,
        in_specs=(
            P("blk", None),
            P(),
            P("blk", "rep", None, None, None),
            P("blk", "rep", None),
            P("blk", "rep"),
            P("blk", None),
        ),
        out_specs=(P("blk", None), P("blk", None), P()),
        check_vma=False,
    )
```

```python
import math

import jax
import jax.numpy as jnp
from jax import lax
from jax.experimental import pallas as pl
from jax.experimental.pallas import tpu as pltpu
from jax.sharding import PartitionSpec as P

MESH = pl.DeviceIdType.MESH
F32, BF16 = jnp.float32, jnp.bfloat16
FEATURES = 512
TILE = 128
TILES = 8
SLOTS = 8
ROWS = 1024
GROUP = 256
GROUPS = ROWS // GROUP
HALVES = 2
WIDTH = FEATURES // HALVES
K0 = math.sqrt(2.0 / math.pi)
K1 = 0.044715


def tile_rows(t):
    return pl.ds(pl.multiple_of(t * TILE, TILE), TILE)


def group_rows(g):
    return pl.ds(pl.multiple_of(g * GROUP, GROUP), GROUP)


def part_rows(p):
    return pl.ds(pl.multiple_of(p * 16, 16), 16)


def half_columns(h):
    return pl.ds(h * WIDTH, WIDTH)


def remote(src, dst, send, recv, blk, rep):
    return pltpu.make_async_remote_copy(
        src_ref=src, dst_ref=dst, send_sem=send, recv_sem=recv,
        device_id=(blk, rep), device_id_type=MESH,
    )


def landed(dst, sem):
    pltpu.make_async_copy(dst, dst, sem).wait()


def dot(a, b):
    return jnp.dot(a, b, preferred_element_type=F32)


def kernel(
    feat, w_in, tiles, slots, counts, cot_in, act_out, gin, gw,
    w, wt, cot, act, tl, tt, inv, invv, invs, dense, denset, ring, blocks, acc, part, parts, agg, back,
    sib_out, sib_in, own_out, heap, total, hop_out, hop_in, grad,
    gw_part, gw_send, gw_recv, gw_half, gw_quarter, gw_ring, gw_fin,
    in_s, out_s,
    t_s, t_r, i_s, i_r, i_l, z_s, z_r, f_s, f_r, s_s, s_r, p_s, p_r, a_s, a_r,
    b_s, b_r, o_s, o_r, h_s, h_r, g_s, g_r,
    wx_s, wx_r, wq_s, wq_r, wz_s, wz_r, wf_s, wf_r, wy_s, wy_r,
):
    b = lax.axis_index("blk")
    r = lax.axis_index("rep")
    z, q = b // 4, b % 4
    yh, core = q // 2, q % 2
    me = yh * 8 + r
    sib = b + 1 - 2 * core
    up = ((z + 1) % 8) * 4 + q
    down = ((z + 7) % 8) * 4 + q
    mine = tile_rows(r)
    low, high = pl.ds(0, TILE // 2), pl.ds(TILE // 2, TILE // 2)

    def plane(y):
        return 4 * z + 2 * y + core

    def along(d):
        return ((z + d) % 8) * 4 + q

    barrier = pltpu.get_barrier_semaphore()
    pl.semaphore_signal(barrier, inc=1, device_id=(sib, r), device_id_type=MESH)

    @pl.loop(1, 8)
    def _(d):
        pl.semaphore_signal(barrier, inc=1, device_id=(along(d), r), device_id_type=MESH)

    @pl.loop(1, 16)
    def _(i):
        p = (me + i) % 16
        pl.semaphore_signal(barrier, inc=1, device_id=(plane(p // 8), p % 8), device_id_type=MESH)

    take_w = pltpu.make_async_copy(w_in, w, in_s.at[0])
    take_w.start()
    take_cot = pltpu.make_async_copy(cot_in, cot, in_s.at[1])
    take_cot.start()
    lane = lax.broadcasted_iota(jnp.int32, (8, TILE), 1)
    for s in range(4):
        index = jnp.full((8, TILE), SLOTS, jnp.int32)
        for k in range(SLOTS):
            index = jnp.where((lane == slots[s, k]) & (k < counts[0, s]), k, index)
        inv[s] = index
    pl.semaphore_wait(barrier, 23)

    sent = []

    def later(what, sem):
        sent.append(lambda: landed(what, sem))

    def peer(i):
        return (me + i) % 16

    def fellow(i):
        return (r + jnp.where(core == 0, i, 8 - i)) % 8

    def giver(i):
        return (r + jnp.where(core == 0, 8 - i, i)) % 8

    def own(h):
        return feat.at[mine, half_columns(h)]

    def shifted(d, y):
        return jnp.where((q == 3) & (y == 0), (d + 1) % 8, d)

    def spread(h, d):
        src = own(h) if d == 0 else ring.at[h, d]
        dst = blocks.at[h, q, mine]
        if d == 0:
            y = 1 - yh
            remote(src, dst, f_s.at[h], f_r.at[h, yh * 4 + r // 2], plane(y), shifted(0, y)).start()

            @pl.when(r == 0)
            def _():
                for s in range(4):
                    rows = pl.ds(s * GROUP, GROUP)
                    pltpu.make_async_copy(
                        feat.at[rows, half_columns(h)], blocks.at[h, q, rows], f_r.at[h, yh * 4 + s]
                    ).start()

            return
        for y in range(2):
            to = shifted(d, y)
            here = (yh == y) & (r == to)

            @pl.when(here)
            def _():
                pltpu.make_async_copy(src, dst, f_r.at[h, yh * 4 + r // 2]).start()

            @pl.when(jnp.logical_not(here))
            def _():
                remote(src, dst, f_s.at[h], f_r.at[h, yh * 4 + r // 2], plane(y), to).start()

    for h in range(HALVES):
        remote(own(h), ring.at[h, 1], z_s.at[h], z_r.at[h, 1], down, r).start()
        remote(own(h), ring.at[h, 7], z_s.at[h], z_r.at[h, 7], up, r).start()
    for m in range(4):
        off = q - 2 + m
        turn = jnp.where(off < -1, -1, jnp.where(off >= 4, 1, 0))
        slot = (off + 4) % 4
        to = (r + turn + 8) % 8

        @pl.when(turn == 0)
        def _():
            pltpu.make_async_copy(tiles.at[m], tl.at[slot, pl.ds(0, SLOTS)], t_r.at[slot]).start()
            pltpu.make_async_copy(inv.at[m], invv.at[slot], i_r.at[slot]).start()

        @pl.when(turn != 0)
        def _():
            remote(tiles.at[m], tl.at[slot, pl.ds(0, SLOTS)], t_s.at[m], t_r.at[slot], b, to).start()
            remote(inv.at[m], invv.at[slot], i_s.at[m], i_r.at[slot], b, to).start()

    def forward_ring(h, k):
        landed(ring.at[h, k], z_r.at[h, k])
        landed(ring.at[h, 8 - k], z_r.at[h, 8 - k])
        if k < 3:
            remote(ring.at[h, k], ring.at[h, k + 1], z_s.at[h], z_r.at[h, k + 1], down, r).start()
            remote(ring.at[h, 8 - k], ring.at[h, 7 - k], z_s.at[h], z_r.at[h, 7 - k], up, r).start()
        else:
            remote(ring.at[h, 3, low], ring.at[h, 4, low], z_s.at[h], z_r.at[h, 4], down, r).start()
            remote(ring.at[h, 5, high], ring.at[h, 4, high], z_s.at[h], z_r.at[h, 0], up, r).start()

    def last_of_ring(h):
        landed(ring.at[h, 4, low], z_r.at[h, 4])
        landed(ring.at[h, 4, high], z_r.at[h, 0])

    spread(0, 0)
    for k in range(1, 4):
        forward_ring(0, k)
        spread(0, k)
        spread(0, 8 - k)
        forward_ring(1, k)
        if k == 2:
            spread(1, 0)
        if k == 3:
            spread(1, 1)
            spread(1, 7)
    last_of_ring(0)
    spread(0, 4)
    for d in (2, 6, 3, 5):
        spread(1, d)
    last_of_ring(1)
    spread(1, 4)
    for h in range(HALVES):
        later(ring.at[h, pl.ds(0, 7)], z_s.at[h])

    def features_sent():
        for count, which in ((15, r == 0), (14, r != 0)):
            @pl.when(which)
            def _():
                for h in range(HALVES):
                    landed(heap.at[h, pl.ds(0, count)], f_s.at[h])

    sent.append(features_sent)

    def lists_sent():
        for m in range(4):
            off = q - 2 + m

            @pl.when((off < -1) | (off >= 4))
            def _():
                landed(tiles.at[m], t_s.at[m])
                landed(inv.at[m], i_s.at[m])

    sent.append(lists_sent)
    take_w.wait()
    wt[...] = w[...].T
    for s in range(4):
        landed(tl.at[s, pl.ds(0, SLOTS)], t_r.at[s])
        landed(invv.at[s], i_r.at[s])
    move = pltpu.make_async_copy(invv, invs, i_l.at[0])
    move.start()
    zero = jnp.zeros((TILE, TILE), BF16)
    for s in range(4):
        tl[s, SLOTS] = zero
        tt[s, SLOTS] = zero

    @pl.loop(0, 4 * SLOTS)
    def _(i):
        tt[i // SLOTS, i % SLOTS] = tl[i // SLOTS, i % SLOTS].T

    move.wait()

    @pl.loop(0, 4 * TILES)
    def _(i):
        s, t = i // TILES, i % TILES
        for c in range(TILES):
            dense[s, tile_rows(t), c * TILE:(c + 1) * TILE] = tl[s, invs[s, 0, t * TILES + c]]
            denset[s, tile_rows(t), c * TILE:(c + 1) * TILE] = tt[s, invs[s, 0, c * TILES + t]]

    take_cot.wait()

    def pass_on(h):
        @pl.loop(0, 8)
        def _(i):
            piece = blocks.at[h, 2 * (i // 4) + core, group_rows(i % 4)]
            landed(piece, f_r.at[h, i])
            remote(piece, piece, s_s.at[h], s_r.at[h], sib, r).start()

        later(heap.at[h], s_s.at[h])

    def own_blocks(h):
        @pl.loop(0, GROUPS)
        def _(g):
            rows = group_rows(g)
            acc[h, rows] = dot(dense[core, rows, :], blocks[h, core]) + dot(
                dense[2 + core, rows, :], blocks[h, 2 + core]
            )

    def sibling_blocks(h):
        landed(heap.at[h], s_r.at[h])

        @pl.loop(0, GROUPS)
        def _(i):
            g = (r // 2 + jnp.where(core == 0, 1 + i, 3 - i)) % GROUPS
            rows = group_rows(g)
            value = dot(dense[1 - core, rows, :], blocks[h, 1 - core]) + dot(
                dense[3 - core, rows, :], blocks[h, 3 - core]
            )
            part[h, rows] = (acc[h, rows] + value).astype(BF16)
            for j in range(2):
                t = 2 * g + j

                @pl.when(t != r)
                def _():
                    remote(part.at[h, tile_rows(t)], parts.at[h, r], p_s.at[h], p_r.at[h], b, t).start()

        later(parts.at[h, pl.ds(0, 7)], p_s.at[h])

    def add_parts(h):
        landed(parts.at[h, pl.ds(0, 7)], p_r.at[h])
        acc[h, 0:TILE] = part[h, mine].astype(F32)

        @pl.loop(1, 8)
        def _(i):
            acc[h, 0:TILE] += parts[h, giver(i)].astype(F32)

        agg[h, mine] = acc[h, 0:TILE].astype(BF16)

    def share(h):
        @pl.loop(1, 8)
        def _(i):
            t = fellow(i)
            remote(agg.at[h, mine], agg.at[h, mine], a_s.at[h], a_r.at[r], b, t).start()

        later(parts.at[h, pl.ds(0, 7)], a_s.at[h])

    pass_on(0)
    own_blocks(0)
    sibling_blocks(0)
    pass_on(1)
    own_blocks(1)
    add_parts(0)
    share(0)
    sibling_blocks(1)
    add_parts(1)
    share(1)

    def chunk(c):
        rows = tile_rows(c)
        pre = dot(agg[0, rows], w[0:WIDTH]) + dot(agg[1, rows], w[WIDTH:])
        square = pre * pre
        t = jnp.tanh(K0 * (pre + K1 * square * pre))
        half = 0.5 * (1.0 + t)
        act[rows] = (pre * half).astype(BF16)
        pltpu.make_async_copy(act.at[rows], act_out.at[rows], out_s.at[0]).start()
        slope = half + 0.5 * pre * (1.0 - t * t) * (K0 * (1.0 + 3.0 * K1 * square))
        delta = (cot[rows].astype(F32) * slope).astype(BF16)
        value = dot(delta, wt[...]).astype(BF16)
        for h in range(HALVES):
            back[h, rows] = value[:, h * WIDTH:(h + 1) * WIDTH]
        return delta

    delta = chunk(r)
    for h in range(HALVES):
        gw_part[h * WIDTH:(h + 1) * WIDTH] = lax.dot_general(
            agg[h, mine], delta, (((0,), (0,)), ((), ())), preferred_element_type=F32
        )
    gw_send[...] = gw_part[group_rows(1 - core)].astype(BF16)
    remote(gw_send, gw_recv, wx_s.at[0], wx_r.at[0], sib, r).start()
    later(gw_send, wx_s.at[0])

    @pl.loop(1, 8)
    def _(i):
        c = giver(i)
        landed(agg.at[0, group_rows(0)], a_r.at[c])
        chunk(c)

    landed(gw_recv, wx_r.at[0])
    gw_half[...] = (gw_part[group_rows(core)] + gw_recv[...].astype(F32)).astype(BF16)

    @pl.loop(1, 16)
    def _(i):
        p = (me + i) % 16
        remote(
            gw_half.at[part_rows(p)], gw_quarter.at[part_rows(me)], wq_s.at[0], wq_r.at[0],
            plane(p // 8), p % 8,
        ).start()

    later(gw_half.at[pl.ds(0, 240)], wq_s.at[0])
    for h in range(HALVES):
        @pl.loop(0, 2 * GROUPS)
        def _(i):
            y, g = i // GROUPS, i % GROUPS
            rows = group_rows(g)
            sib_out[h, y, rows] = dot(denset[2 * y + 1 - core, rows, :], back[h]).astype(BF16)
            remote(
                sib_out.at[h, y, rows], sib_in.at[h, y, rows], b_s.at[h], b_r.at[h, i], sib, r
            ).start()

        later(sib_out.at[h], b_s.at[h])

    def own_grads(h):
        @pl.loop(0, 2 * GROUPS)
        def _(i):
            j = i % 4
            y, g = (i + i // 4) % 2, (r // 2 + 2 * j + 1 + 5 * (j // 2)) % GROUPS
            rows = group_rows(g)
            value = dot(denset[2 * y + core, rows, :], back[h])
            landed(sib_in.at[h, y, rows], b_r.at[h, y * GROUPS + g])
            own_out[h, y, rows] = (value + sib_in[h, y, rows].astype(F32)).astype(BF16)
            for j in range(2):
                t = 2 * g + j
                src, dst = own_out.at[h, y, tile_rows(t)], heap.at[h, me]
                turned = jnp.where((yh == 0) & (core == 1) & (y == 1), (r + 7) % 8, r)
                here = (yh == y) & (r == t)

                @pl.when(here)
                def _():
                    pltpu.make_async_copy(src, dst, o_r.at[h, turned]).start()

                @pl.when(jnp.logical_not(here))
                def _():
                    remote(src, dst, o_s.at[h], o_r.at[h, turned], plane(y), t).start()

        later(heap.at[h, pl.ds(0, 15)], o_s.at[h])

    own_grads(0)
    own_grads(1)
    landed(gw_quarter.at[pl.ds(0, 240)], wq_r.at[0])
    gw_ring[0] = gw_half[part_rows(me)].astype(F32)

    @pl.loop(1, 16)
    def _(i):
        p = (me + i) % 16
        gw_ring[0] += gw_quarter[part_rows(p)].astype(F32)

    @pl.loop(1, 8)
    def _(d):
        remote(gw_ring.at[0], gw_ring.at[d], wz_s.at[0], wz_r.at[0], along(d), r).start()

    later(gw_ring.at[pl.ds(0, 7)], wz_s.at[0])

    def send_along(h):
        @pl.loop(0, 8)
        def _(i):
            d = 2 * ((r // 2 + 7 - i // 2 - 2 * yh) % 4) + i % 2
            first = shifted(d, 0)
            landed(heap.at[h, pl.ds(0, 2)], o_r.at[h, d])
            value = heap[h, first].astype(F32) + heap[h, 8 + d].astype(F32)

            @pl.when(d == 0)
            def _():
                total[h] = value

            @pl.when(d != 0)
            def _():
                hop_out[h, d] = value.astype(BF16)
                remote(hop_out.at[h, d], hop_in.at[h, d], h_s.at[h], h_r.at[h], along(d), r).start()

        later(ring.at[h, pl.ds(0, 7)], h_s.at[h])

    def finish(h):
        landed(hop_in.at[h, pl.ds(0, 7)], h_r.at[h])

        @pl.loop(1, 8)
        def _(d):
            total[h] += hop_in[h, d].astype(F32)

        place = grad.at[h, mine]
        grad[h, mine] = total[h].astype(BF16)

        @pl.loop(1, 8)
        def _(i):
            t = fellow(i)
            remote(place, place, g_s.at[h], g_r.at[h], b, t).start()

        later(parts.at[h, pl.ds(0, 7)], g_s.at[h])

    send_along(0)
    landed(gw_ring.at[pl.ds(0, 7)], wz_r.at[0])

    whole = gw_ring[z]
    for k in range(1, 8):
        whole = whole + gw_ring[(z + 8 - k) % 8]
    place = pl.ds(pl.multiple_of(core * 256 + me * 16, 16), 16)
    gw_fin[place] = (whole * (1.0 / math.sqrt(32 * ROWS))).astype(BF16)

    @pl.loop(1, 16)
    def _(i):
        p = (me + i) % 16
        remote(
            gw_fin.at[place], gw_fin.at[place], wf_s.at[0], wf_r.at[0], plane(p // 8), p % 8
        ).start()

    later(gw_half.at[pl.ds(0, 240)], wf_s.at[0])

    finish(0)
    send_along(1)
    finish(1)

    landed(gw_fin.at[pl.ds(0, 240)], wf_r.at[0])
    landed(act, out_s.at[0])

    half = group_rows(core)
    remote(gw_fin.at[half], gw_fin.at[half], wy_s.at[0], wy_r.at[0], sib, r).start()
    later(gw_fin.at[half], wy_s.at[0])
    landed(gw_fin.at[group_rows(1 - core)], wy_r.at[0])
    give_gw = pltpu.make_async_copy(gw_fin, gw, in_s.at[0])
    give_gw.start()

    for h in range(HALVES):
        landed(parts.at[h, pl.ds(0, 7)], g_r.at[h])
        pltpu.make_async_copy(grad.at[h], gin.at[:, half_columns(h)], out_s.at[h]).start()

    for wait in sent:
        wait()
    give_gw.wait()
    for h in range(HALVES):
        landed(grad.at[h], out_s.at[h])


def per_device(features, layer_weight, adjacency_tiles, tile_slots, tile_counts, cotangent):
    hbm = pl.BlockSpec(memory_space=pl.ANY)
    smem = pl.BlockSpec(memory_space=pltpu.SMEM)
    dma = pltpu.SemaphoreType.DMA
    half = (HALVES, ROWS, WIDTH)
    slices = (HALVES, 8, TILE, WIDTH)
    scratch = [
        pltpu.VMEM((FEATURES, FEATURES), BF16),
        pltpu.VMEM((FEATURES, FEATURES), BF16),
        pltpu.VMEM((ROWS, FEATURES), BF16),
        pltpu.VMEM((ROWS, FEATURES), BF16),
        pltpu.VMEM((4, SLOTS + 1, TILE, TILE), BF16),
        pltpu.VMEM((4, SLOTS + 1, TILE, TILE), BF16),
        pltpu.VMEM((4, 8, TILE), jnp.int32),
        pltpu.VMEM((4, 8, TILE), jnp.int32),
        pltpu.SMEM((4, 8, TILE), jnp.int32),
        pltpu.VMEM((4, ROWS, ROWS), BF16),
        pltpu.VMEM((4, ROWS, ROWS), BF16),
        pltpu.VMEM(slices, BF16),
        pltpu.VMEM((HALVES, 4, ROWS, WIDTH), BF16),
        pltpu.VMEM(half, F32),
        pltpu.VMEM(half, BF16),
        pltpu.VMEM(slices, BF16),
        pltpu.VMEM(half, BF16),
        pltpu.VMEM(half, BF16),
        pltpu.VMEM((HALVES, 2, ROWS, WIDTH), BF16),
        pltpu.VMEM((HALVES, 2, ROWS, WIDTH), BF16),
        pltpu.VMEM((HALVES, 2, ROWS, WIDTH), BF16),
        pltpu.VMEM((HALVES, 16, TILE, WIDTH), BF16),
        pltpu.VMEM((HALVES, TILE, WIDTH), F32),
        pltpu.VMEM(slices, BF16),
        pltpu.VMEM(slices, BF16),
        pltpu.VMEM(half, BF16),
        pltpu.VMEM((FEATURES, FEATURES), F32),
        pltpu.VMEM((256, FEATURES), BF16),
        pltpu.VMEM((256, FEATURES), BF16),
        pltpu.VMEM((256, FEATURES), BF16),
        pltpu.VMEM((256, FEATURES), BF16),
        pltpu.VMEM((8, 16, FEATURES), F32),
        pltpu.VMEM((FEATURES, FEATURES), BF16),
    ]
    two = HALVES
    two = (HALVES,)
    sems = [
        (2,), (HALVES,),
        (4,), (4,), (4,), (4,), (1,),
        two, (HALVES, 8), two, (HALVES, 8), two, two,
        two, two, two, (8,),
        two, (HALVES, 8), two, (HALVES, 8), two, two, two, two,
        (1,), (1,), (1,), (1,), (1,), (1,), (1,), (1,), (1,), (1,),
    ]
    activated, grad_input, grad_weight = pl.pallas_call(
        kernel,
        out_shape=(
            jax.ShapeDtypeStruct((ROWS, FEATURES), BF16),
            jax.ShapeDtypeStruct((ROWS, FEATURES), BF16),
            jax.ShapeDtypeStruct((FEATURES, FEATURES), BF16),
        ),
        in_specs=[hbm, hbm, hbm, smem, smem, hbm],
        out_specs=(hbm, hbm, hbm),
        scratch_shapes=scratch + [dma(n) for n in sems],
        compiler_params=pltpu.CompilerParams(
            collective_id=0, has_side_effects=True, vmem_limit_bytes=58 * 1024 * 1024
        ),
        cost_estimate=pl.CostEstimate(
            flops=10 * 2 * ROWS * ROWS * FEATURES, bytes_accessed=8 << 20, transcendentals=ROWS * FEATURES
        ),
    )(features, layer_weight, adjacency_tiles[0], tile_slots[0], tile_counts, cotangent)
    return activated, grad_input, grad_weight.astype(F32)


def solution(mesh):
    return jax.shard_map(
        per_device,
        mesh=mesh,
        in_specs=(
            P("blk", None),
            P(),
            P("blk", "rep", None, None, None),
            P("blk", "rep", None),
            P("blk", "rep"),
            P("blk", None),
        ),
        out_specs=(P("blk", None), P("blk", None), P()),
        check_vma=False,
    )
```

```python
import math

import jax
import jax.numpy as jnp
from jax import lax
from jax.experimental import pallas as pl
from jax.experimental.pallas import tpu as pltpu
from jax.sharding import PartitionSpec as P

MESH = pl.DeviceIdType.MESH
F32, BF16 = jnp.float32, jnp.bfloat16
FEATURES = 512
TILE = 128
TILES = 8
SLOTS = 8
ROWS = 1024
GROUP = 256
GROUPS = ROWS // GROUP
PARTS = 4
WIDTH = FEATURES // PARTS
K0 = math.sqrt(2.0 / math.pi)
K1 = 0.044715


def tile_rows(t):
    return pl.ds(pl.multiple_of(t * TILE, TILE), TILE)


def group_rows(g):
    return pl.ds(pl.multiple_of(g * GROUP, GROUP), GROUP)


def part_rows(p):
    return pl.ds(pl.multiple_of(p * 16, 16), 16)


def columns_of(h):
    return pl.ds(h * WIDTH, WIDTH)


def remote(src, dst, send, recv, blk, rep):
    return pltpu.make_async_remote_copy(
        src_ref=src, dst_ref=dst, send_sem=send, recv_sem=recv,
        device_id=(blk, rep), device_id_type=MESH,
    )


def landed(dst, sem):
    pltpu.make_async_copy(dst, dst, sem).wait()


def dot(a, b):
    return jnp.dot(a, b, preferred_element_type=F32)


def kernel(
    feat, w_in, tiles, slots, counts, cot_in, act_out, gin, gw,
    w, wt, cot, act, tl, tt, inv, invv, invs, dense, denset, ring, blocks, acc, part, parts, agg, back,
    sib_out, sib_in, own_out, heap, total, hop_out, hop_in, grad,
    gw_part, gw_send, gw_recv, gw_half, gw_quarter, gw_ring, gw_fin,
    in_s, out_s,
    t_s, t_r, i_s, i_r, i_l, z_s, z_r, f_s, f_r, s_s, s_r, p_s, p_r, a_s, a_r,
    b_s, b_r, o_s, o_r, h_s, h_r, g_s, g_r,
    wx_s, wx_r, wq_s, wq_r, wz_s, wz_r, wf_s, wf_r, wy_s, wy_r,
):
    b = lax.axis_index("blk")
    r = lax.axis_index("rep")
    z, q = b // 4, b % 4
    yh, core = q // 2, q % 2
    me = yh * 8 + r
    sib = b + 1 - 2 * core
    up = ((z + 1) % 8) * 4 + q
    down = ((z + 7) % 8) * 4 + q
    mine = tile_rows(r)
    low, high = pl.ds(0, TILE // 2), pl.ds(TILE // 2, TILE // 2)

    def plane(y):
        return 4 * z + 2 * y + core

    def along(d):
        return ((z + d) % 8) * 4 + q

    barrier = pltpu.get_barrier_semaphore()
    pl.semaphore_signal(barrier, inc=1, device_id=(sib, r), device_id_type=MESH)

    @pl.loop(1, 8)
    def _(d):
        pl.semaphore_signal(barrier, inc=1, device_id=(along(d), r), device_id_type=MESH)

    @pl.loop(1, 16)
    def _(i):
        p = (me + i) % 16
        pl.semaphore_signal(barrier, inc=1, device_id=(plane(p // 8), p % 8), device_id_type=MESH)

    take_w = pltpu.make_async_copy(w_in, w, in_s.at[0])
    take_w.start()
    take_cot = pltpu.make_async_copy(cot_in, cot, in_s.at[1])
    take_cot.start()
    lane = lax.broadcasted_iota(jnp.int32, (8, TILE), 1)
    for s in range(4):
        index = jnp.full((8, TILE), SLOTS, jnp.int32)
        for k in range(SLOTS):
            index = jnp.where((lane == slots[s, k]) & (k < counts[0, s]), k, index)
        inv[s] = index
    pl.semaphore_wait(barrier, 23)

    sent = []

    def later(what, sem):
        sent.append(lambda: landed(what, sem))

    def peer(i):
        return (me + i) % 16

    def fellow(i):
        return (r + jnp.where(core == 0, i, 8 - i)) % 8

    def giver(i):
        return (r + jnp.where(core == 0, 8 - i, i)) % 8

    def own(h):
        return feat.at[mine, columns_of(h)]

    def shifted(d, y):
        return jnp.where((q == 3) & (y == 0), (d + 1) % 8, d)

    def spread(h, d):
        src = own(h) if d == 0 else ring.at[h, d]
        dst = blocks.at[h, q, mine]
        if d == 0:
            y = 1 - yh
            remote(src, dst, f_s.at[h], f_r.at[h, yh * 4 + r // 2], plane(y), shifted(0, y)).start()

            @pl.when(r == 0)
            def _():
                for s in range(4):
                    rows = pl.ds(s * GROUP, GROUP)
                    pltpu.make_async_copy(
                        feat.at[rows, columns_of(h)], blocks.at[h, q, rows], f_r.at[h, yh * 4 + s]
                    ).start()

            return
        for y in range(2):
            to = shifted(d, y)
            here = (yh == y) & (r == to)

            @pl.when(here)
            def _():
                pltpu.make_async_copy(src, dst, f_r.at[h, yh * 4 + r // 2]).start()

            @pl.when(jnp.logical_not(here))
            def _():
                remote(src, dst, f_s.at[h], f_r.at[h, yh * 4 + r // 2], plane(y), to).start()

    for h in range(PARTS):
        remote(own(h), ring.at[h, 1], z_s.at[h], z_r.at[h, 1], down, r).start()
        remote(own(h), ring.at[h, 7], z_s.at[h], z_r.at[h, 7], up, r).start()
    for m in range(4):
        off = q - 2 + m
        turn = jnp.where(off < -1, -1, jnp.where(off >= 4, 1, 0))
        slot = (off + 4) % 4
        to = (r + turn + 8) % 8

        @pl.when(turn == 0)
        def _():
            pltpu.make_async_copy(tiles.at[m], tl.at[slot, pl.ds(0, SLOTS)], t_r.at[slot]).start()
            pltpu.make_async_copy(inv.at[m], invv.at[slot], i_r.at[slot]).start()

        @pl.when(turn != 0)
        def _():
            remote(tiles.at[m], tl.at[slot, pl.ds(0, SLOTS)], t_s.at[m], t_r.at[slot], b, to).start()
            remote(inv.at[m], invv.at[slot], i_s.at[m], i_r.at[slot], b, to).start()

    def forward_ring(h, k):
        landed(ring.at[h, k], z_r.at[h, k])
        landed(ring.at[h, 8 - k], z_r.at[h, 8 - k])
        if k < 3:
            remote(ring.at[h, k], ring.at[h, k + 1], z_s.at[h], z_r.at[h, k + 1], down, r).start()
            remote(ring.at[h, 8 - k], ring.at[h, 7 - k], z_s.at[h], z_r.at[h, 7 - k], up, r).start()
        else:
            remote(ring.at[h, 3, low], ring.at[h, 4, low], z_s.at[h], z_r.at[h, 4], down, r).start()
            remote(ring.at[h, 5, high], ring.at[h, 4, high], z_s.at[h], z_r.at[h, 0], up, r).start()

    def last_of_ring(h):
        landed(ring.at[h, 4, low], z_r.at[h, 4])
        landed(ring.at[h, 4, high], z_r.at[h, 0])

    for turn in range(PARTS + 4):
        for h in range(PARTS):
            k = turn - h
            if k == 0:
                spread(h, 0)
            elif 1 <= k <= 3:
                forward_ring(h, k)
                spread(h, k)
                spread(h, 8 - k)
            elif k == 4:
                last_of_ring(h)
                spread(h, 4)
    for h in range(PARTS):
        later(ring.at[h, pl.ds(0, 7)], z_s.at[h])

    def features_sent():
        for count, which in ((15, r == 0), (14, r != 0)):
            @pl.when(which)
            def _():
                for h in range(PARTS):
                    landed(heap.at[h, pl.ds(0, count)], f_s.at[h])

    sent.append(features_sent)

    def lists_sent():
        for m in range(4):
            off = q - 2 + m

            @pl.when((off < -1) | (off >= 4))
            def _():
                landed(tiles.at[m], t_s.at[m])
                landed(inv.at[m], i_s.at[m])

    sent.append(lists_sent)
    take_w.wait()
    wt[...] = w[...].T
    for s in range(4):
        landed(tl.at[s, pl.ds(0, SLOTS)], t_r.at[s])
        landed(invv.at[s], i_r.at[s])
    move = pltpu.make_async_copy(invv, invs, i_l.at[0])
    move.start()
    zero = jnp.zeros((TILE, TILE), BF16)
    for s in range(4):
        tl[s, SLOTS] = zero
        tt[s, SLOTS] = zero

    @pl.loop(0, 4 * SLOTS)
    def _(i):
        tt[i // SLOTS, i % SLOTS] = tl[i // SLOTS, i % SLOTS].T

    move.wait()

    @pl.loop(0, 4 * TILES)
    def _(i):
        s, t = i // TILES, i % TILES
        for c in range(TILES):
            dense[s, tile_rows(t), c * TILE:(c + 1) * TILE] = tl[s, invs[s, 0, t * TILES + c]]
            denset[s, tile_rows(t), c * TILE:(c + 1) * TILE] = tt[s, invs[s, 0, c * TILES + t]]

    take_cot.wait()

    def pass_on(h):
        @pl.loop(0, 8)
        def _(i):
            piece = blocks.at[h, 2 * (i // 4) + core, group_rows(i % 4)]
            landed(piece, f_r.at[h, i])
            remote(piece, piece, s_s.at[h], s_r.at[h], sib, r).start()

        later(heap.at[h], s_s.at[h])

    def own_blocks(h):
        @pl.loop(0, GROUPS)
        def _(g):
            rows = group_rows(g)
            acc[h, rows] = dot(dense[core, rows, :], blocks[h, core]) + dot(
                dense[2 + core, rows, :], blocks[h, 2 + core]
            )

    def sibling_blocks(h):
        landed(heap.at[h], s_r.at[h])

        @pl.loop(0, GROUPS)
        def _(i):
            g = (r // 2 + jnp.where(core == 0, 1 + i, 3 - i)) % GROUPS
            rows = group_rows(g)
            value = dot(dense[1 - core, rows, :], blocks[h, 1 - core]) + dot(
                dense[3 - core, rows, :], blocks[h, 3 - core]
            )
            part[h, rows] = (acc[h, rows] + value).astype(BF16)
            for j in range(2):
                t = 2 * g + j

                @pl.when(t != r)
                def _():
                    remote(part.at[h, tile_rows(t)], parts.at[h, r], p_s.at[h], p_r.at[h], b, t).start()

        later(parts.at[h, pl.ds(0, 7)], p_s.at[h])

    def add_parts(h):
        landed(parts.at[h, pl.ds(0, 7)], p_r.at[h])
        acc[h, 0:TILE] = part[h, mine].astype(F32)

        @pl.loop(1, 8)
        def _(i):
            acc[h, 0:TILE] += parts[h, giver(i)].astype(F32)

        agg[h, mine] = acc[h, 0:TILE].astype(BF16)

    def share(h):
        @pl.loop(1, 8)
        def _(i):
            t = fellow(i)
            remote(agg.at[h, mine], agg.at[h, mine], a_s.at[h], a_r.at[r], b, t).start()

        later(parts.at[h, pl.ds(0, 7)], a_s.at[h])

    for h in range(PARTS):
        pass_on(h)
        own_blocks(h)
        if h >= 2:
            add_parts(h - 2)
            share(h - 2)
        sibling_blocks(h)
    for h in range(PARTS - 2, PARTS):
        add_parts(h)
        share(h)

    def chunk(c):
        rows = tile_rows(c)
        inputs = jnp.concatenate([agg[h, rows] for h in range(PARTS)], axis=1)
        pre = dot(inputs, w[...])
        square = pre * pre
        t = jnp.tanh(K0 * (pre + K1 * square * pre))
        half = 0.5 * (1.0 + t)
        act[rows] = (pre * half).astype(BF16)
        pltpu.make_async_copy(act.at[rows], act_out.at[rows], out_s.at[0]).start()
        slope = half + 0.5 * pre * (1.0 - t * t) * (K0 * (1.0 + 3.0 * K1 * square))
        delta = (cot[rows].astype(F32) * slope).astype(BF16)
        value = dot(delta, wt[...]).astype(BF16)
        for h in range(PARTS):
            back[h, rows] = value[:, h * WIDTH:(h + 1) * WIDTH]
        return inputs, delta

    gw_part[...] = lax.dot_general(
        *chunk(r), (((0,), (0,)), ((), ())), preferred_element_type=F32
    )
    gw_send[...] = gw_part[group_rows(1 - core)].astype(BF16)
    remote(gw_send, gw_recv, wx_s.at[0], wx_r.at[0], sib, r).start()
    later(gw_send, wx_s.at[0])

    @pl.loop(1, 8)
    def _(i):
        c = giver(i)
        landed(agg.at[0, pl.ds(0, PARTS * TILE)], a_r.at[c])
        chunk(c)

    landed(gw_recv, wx_r.at[0])
    gw_half[...] = (gw_part[group_rows(core)] + gw_recv[...].astype(F32)).astype(BF16)

    @pl.loop(1, 16)
    def _(i):
        p = (me + i) % 16
        remote(
            gw_half.at[part_rows(p)], gw_quarter.at[part_rows(me)], wq_s.at[0], wq_r.at[0],
            plane(p // 8), p % 8,
        ).start()

    later(gw_half.at[pl.ds(0, 240)], wq_s.at[0])
    def sibling_grads(h):
        @pl.loop(0, 2 * GROUPS)
        def _(i):
            y, g = i // GROUPS, i % GROUPS
            rows = group_rows(g)
            sib_out[h, y, rows] = dot(denset[2 * y + 1 - core, rows, :], back[h]).astype(BF16)
            remote(
                sib_out.at[h, y, rows], sib_in.at[h, y, rows], b_s.at[h], b_r.at[h], sib, r
            ).start()

        later(sib_out.at[h], b_s.at[h])

    def own_grads(h):
        landed(sib_in.at[h], b_r.at[h])

        @pl.loop(0, 2 * GROUPS)
        def _(i):
            j = i % 4
            y, g = (i + i // 4) % 2, (r // 2 + 2 * j + 1 + 5 * (j // 2)) % GROUPS
            rows = group_rows(g)
            value = dot(denset[2 * y + core, rows, :], back[h])
            own_out[h, y, rows] = (value + sib_in[h, y, rows].astype(F32)).astype(BF16)
            for j in range(2):
                t = 2 * g + j
                src, dst = own_out.at[h, y, tile_rows(t)], heap.at[h, me]
                turned = jnp.where((yh == 0) & (core == 1) & (y == 1), (r + 7) % 8, r)
                here = (yh == y) & (r == t)

                @pl.when(here)
                def _():
                    pltpu.make_async_copy(src, dst, o_r.at[h, turned]).start()

                @pl.when(jnp.logical_not(here))
                def _():
                    remote(src, dst, o_s.at[h], o_r.at[h, turned], plane(y), t).start()

        later(heap.at[h, pl.ds(0, 15)], o_s.at[h])

    sibling_grads(0)
    sibling_grads(1)
    for h in range(PARTS):
        own_grads(h)
        if h + 2 < PARTS:
            sibling_grads(h + 2)
    landed(gw_quarter.at[pl.ds(0, 240)], wq_r.at[0])
    gw_ring[0] = gw_half[part_rows(me)].astype(F32)

    @pl.loop(1, 16)
    def _(i):
        p = (me + i) % 16
        gw_ring[0] += gw_quarter[part_rows(p)].astype(F32)

    @pl.loop(1, 8)
    def _(d):
        remote(gw_ring.at[0], gw_ring.at[d], wz_s.at[0], wz_r.at[0], along(d), r).start()

    later(gw_ring.at[pl.ds(0, 7)], wz_s.at[0])

    def send_along(h):
        @pl.loop(0, 8)
        def _(i):
            d = 2 * ((r // 2 + 7 - i // 2 - 2 * yh) % 4) + i % 2
            first = shifted(d, 0)
            landed(heap.at[h, pl.ds(0, 2)], o_r.at[h, d])
            value = heap[h, first].astype(F32) + heap[h, 8 + d].astype(F32)

            @pl.when(d == 0)
            def _():
                total[h] = value

            @pl.when(d != 0)
            def _():
                hop_out[h, d] = value.astype(BF16)
                remote(hop_out.at[h, d], hop_in.at[h, d], h_s.at[h], h_r.at[h], along(d), r).start()

        later(ring.at[h, pl.ds(0, 7)], h_s.at[h])

    def finish(h):
        landed(hop_in.at[h, pl.ds(0, 7)], h_r.at[h])

        @pl.loop(1, 8)
        def _(d):
            total[h] += hop_in[h, d].astype(F32)

        place = grad.at[h, mine]
        grad[h, mine] = total[h].astype(BF16)

        @pl.loop(1, 8)
        def _(i):
            t = fellow(i)
            remote(place, place, g_s.at[h], g_r.at[h], b, t).start()

        later(parts.at[h, pl.ds(0, 7)], g_s.at[h])

    send_along(0)
    send_along(1)
    landed(gw_ring.at[pl.ds(0, 7)], wz_r.at[0])

    whole = gw_ring[z]
    for k in range(1, 8):
        whole = whole + gw_ring[(z + 8 - k) % 8]
    place = pl.ds(pl.multiple_of(core * 256 + me * 16, 16), 16)
    gw_fin[place] = (whole * (1.0 / math.sqrt(32 * ROWS))).astype(BF16)

    @pl.loop(1, 16)
    def _(i):
        p = (me + i) % 16
        remote(
            gw_fin.at[place], gw_fin.at[place], wf_s.at[0], wf_r.at[0], plane(p // 8), p % 8
        ).start()

    later(gw_half.at[pl.ds(0, 240)], wf_s.at[0])

    for h in range(PARTS):
        finish(h)
        if h + 2 < PARTS:
            send_along(h + 2)

    landed(gw_fin.at[pl.ds(0, 240)], wf_r.at[0])
    landed(act, out_s.at[0])

    half = group_rows(core)
    remote(gw_fin.at[half], gw_fin.at[half], wy_s.at[0], wy_r.at[0], sib, r).start()
    later(gw_fin.at[half], wy_s.at[0])
    landed(gw_fin.at[group_rows(1 - core)], wy_r.at[0])
    give_gw = pltpu.make_async_copy(gw_fin, gw, in_s.at[0])
    give_gw.start()

    for h in range(PARTS):
        landed(parts.at[h, pl.ds(0, 7)], g_r.at[h])
        pltpu.make_async_copy(grad.at[h], gin.at[:, columns_of(h)], out_s.at[h]).start()

    for wait in sent:
        wait()
    give_gw.wait()
    for h in range(PARTS):
        landed(grad.at[h], out_s.at[h])


def hand_over_kernel(act, grad, weight, act_out, grad_out, weight_out, held, narrow, wide, get, give):
    rows = ROWS // 4
    gets, gives = [], []
    for n, (src, dst) in enumerate(((act, act_out), (grad, grad_out))):
        for m in range(4):
            part, place = pl.ds(m * rows, rows), held.at[4 * n + m]
            gets.append(pltpu.make_async_copy(src.at[part], place, get.at[4 * n + m]))
            gives.append(pltpu.make_async_copy(place, dst.at[part], give.at[4 * n + m]))
    take = pltpu.make_async_copy(weight, narrow, get.at[8])
    take.start()
    for copy in gets:
        copy.start()
    take.wait()
    wide[...] = narrow[...].astype(F32)
    put = pltpu.make_async_copy(wide, weight_out, give.at[8])
    put.start()
    for first, second in zip(gets, gives):
        first.wait()
        second.start()
    for copy in gives:
        copy.wait()
    put.wait()


def hand_over(act, grad, weight):
    hbm = pl.BlockSpec(memory_space=pl.ANY)
    return pl.pallas_call(
        hand_over_kernel,
        out_shape=(
            jax.ShapeDtypeStruct((ROWS, FEATURES), BF16),
            jax.ShapeDtypeStruct((ROWS, FEATURES), BF16),
            jax.ShapeDtypeStruct((FEATURES, FEATURES), F32),
        ),
        in_specs=[hbm, hbm, hbm],
        out_specs=(hbm, hbm, hbm),
        scratch_shapes=[
            pltpu.VMEM((8, ROWS // 4, FEATURES), BF16),
            pltpu.VMEM((FEATURES, FEATURES), BF16),
            pltpu.VMEM((FEATURES, FEATURES), F32),
            pltpu.SemaphoreType.DMA((9,)),
            pltpu.SemaphoreType.DMA((9,)),
        ],
        compiler_params=pltpu.CompilerParams(vmem_limit_bytes=60 * 1024 * 1024),
        cost_estimate=pl.CostEstimate(flops=0, bytes_accessed=6 << 20, transcendentals=0),
    )(act, grad, weight)


def per_device(features, layer_weight, adjacency_tiles, tile_slots, tile_counts, cotangent):
    hbm = pl.BlockSpec(memory_space=pl.ANY)
    smem = pl.BlockSpec(memory_space=pltpu.SMEM)
    dma = pltpu.SemaphoreType.DMA
    half = (PARTS, ROWS, WIDTH)
    slices = (PARTS, 8, TILE, WIDTH)
    scratch = [
        pltpu.VMEM((FEATURES, FEATURES), BF16),
        pltpu.VMEM((FEATURES, FEATURES), BF16),
        pltpu.VMEM((ROWS, FEATURES), BF16),
        pltpu.VMEM((ROWS, FEATURES), BF16),
        pltpu.VMEM((4, SLOTS + 1, TILE, TILE), BF16),
        pltpu.VMEM((4, SLOTS + 1, TILE, TILE), BF16),
        pltpu.VMEM((4, 8, TILE), jnp.int32),
        pltpu.VMEM((4, 8, TILE), jnp.int32),
        pltpu.SMEM((4, 8, TILE), jnp.int32),
        pltpu.VMEM((4, ROWS, ROWS), BF16),
        pltpu.VMEM((4, ROWS, ROWS), BF16),
        pltpu.VMEM(slices, BF16),
        pltpu.VMEM((PARTS, 4, ROWS, WIDTH), BF16),
        pltpu.VMEM(half, F32),
        pltpu.VMEM(half, BF16),
        pltpu.VMEM(slices, BF16),
        pltpu.VMEM(half, BF16),
        pltpu.VMEM(half, BF16),
        pltpu.VMEM((PARTS, 2, ROWS, WIDTH), BF16),
        pltpu.VMEM((PARTS, 2, ROWS, WIDTH), BF16),
        pltpu.VMEM((PARTS, 2, ROWS, WIDTH), BF16),
        pltpu.VMEM((PARTS, 16, TILE, WIDTH), BF16),
        pltpu.VMEM((PARTS, TILE, WIDTH), F32),
        pltpu.VMEM(slices, BF16),
        pltpu.VMEM(slices, BF16),
        pltpu.VMEM(half, BF16),
        pltpu.VMEM((FEATURES, FEATURES), F32),
        pltpu.VMEM((256, FEATURES), BF16),
        pltpu.VMEM((256, FEATURES), BF16),
        pltpu.VMEM((256, FEATURES), BF16),
        pltpu.VMEM((256, FEATURES), BF16),
        pltpu.VMEM((8, 16, FEATURES), F32),
        pltpu.VMEM((FEATURES, FEATURES), BF16),
    ]
    two = PARTS
    two = (PARTS,)
    sems = [
        (2,), (PARTS,),
        (4,), (4,), (4,), (4,), (1,),
        two, (PARTS, 8), two, (PARTS, 8), two, two,
        two, two, two, (8,),
        two, two, two, (PARTS, 8), two, two, two, two,
        (1,), (1,), (1,), (1,), (1,), (1,), (1,), (1,), (1,), (1,),
    ]
    activated, grad_input, grad_weight = pl.pallas_call(
        kernel,
        out_shape=(
            jax.ShapeDtypeStruct((ROWS, FEATURES), BF16),
            jax.ShapeDtypeStruct((ROWS, FEATURES), BF16),
            jax.ShapeDtypeStruct((FEATURES, FEATURES), BF16),
        ),
        in_specs=[hbm, hbm, hbm, smem, smem, hbm],
        out_specs=(hbm, hbm, hbm),
        scratch_shapes=scratch + [dma(n) for n in sems],
        compiler_params=pltpu.CompilerParams(
            collective_id=0, has_side_effects=True, vmem_limit_bytes=58 * 1024 * 1024
        ),
        cost_estimate=pl.CostEstimate(
            flops=10 * 2 * ROWS * ROWS * FEATURES, bytes_accessed=8 << 20, transcendentals=ROWS * FEATURES
        ),
    )(features, layer_weight, adjacency_tiles[0], tile_slots[0], tile_counts, cotangent)
    return hand_over(activated, grad_input, grad_weight)


def solution(mesh):
    return jax.shard_map(
        per_device,
        mesh=mesh,
        in_specs=(
            P("blk", None),
            P(),
            P("blk", "rep", None, None, None),
            P("blk", "rep", None),
            P("blk", "rep"),
            P("blk", None),
        ),
        out_specs=(P("blk", None), P("blk", None), P()),
        check_vma=False,
    )
```

```python
import math

import jax
import jax.numpy as jnp
from jax import lax
from jax.experimental import pallas as pl
from jax.experimental.pallas import tpu as pltpu
from jax.sharding import PartitionSpec as P

MESH = pl.DeviceIdType.MESH
F32, BF16 = jnp.float32, jnp.bfloat16
FEATURES = 512
TILE = 128
TILES = 8
SLOTS = 8
ROWS = 1024
GROUP = 256
GROUPS = ROWS // GROUP
PARTS = 4
WIDTH = FEATURES // PARTS
K0 = math.sqrt(2.0 / math.pi)
K1 = 0.044715


def tile_rows(t):
    return pl.ds(pl.multiple_of(t * TILE, TILE), TILE)


def group_rows(g):
    return pl.ds(pl.multiple_of(g * GROUP, GROUP), GROUP)


def part_rows(p):
    return pl.ds(pl.multiple_of(p * 16, 16), 16)


def columns_of(h):
    return pl.ds(h * WIDTH, WIDTH)


def remote(src, dst, send, recv, blk, rep):
    return pltpu.make_async_remote_copy(
        src_ref=src, dst_ref=dst, send_sem=send, recv_sem=recv,
        device_id=(blk, rep), device_id_type=MESH,
    )


def landed(dst, sem):
    pltpu.make_async_copy(dst, dst, sem).wait()


def dot(a, b):
    return jnp.dot(a, b, preferred_element_type=F32)


def kernel(
    feat, w_in, tiles, slots, counts, cot_in, act_out, gin, gw,
    w, wt, cot, act, tl, tt, inv, invv, invs, dense, denset, ring, blocks, acc, part, parts, agg, back,
    sib_out, sib_in, own_out, heap, total, hop_out, hop_in, grad,
    gw_part, gw_send, gw_recv, gw_half, gw_quarter, gw_ring, gw_fin,
    in_s, out_s,
    t_s, t_r, i_s, i_r, i_l, z_s, z_r, f_s, f_r, s_s, s_r, p_s, p_r, a_s, a_r,
    b_s, b_r, o_s, o_r, h_s, h_r, g_s, g_r,
    wx_s, wx_r, wq_s, wq_r, wz_s, wz_r, wf_s, wf_r, wy_s, wy_r,
):
    b = lax.axis_index("blk")
    r = lax.axis_index("rep")
    z, q = b // 4, b % 4
    yh, core = q // 2, q % 2
    me = yh * 8 + r
    sib = b + 1 - 2 * core
    up = ((z + 1) % 8) * 4 + q
    down = ((z + 7) % 8) * 4 + q
    mine = tile_rows(r)
    low, high = pl.ds(0, TILE // 2), pl.ds(TILE // 2, TILE // 2)

    def plane(y):
        return 4 * z + 2 * y + core

    def along(d):
        return ((z + d) % 8) * 4 + q

    barrier = pltpu.get_barrier_semaphore()
    pl.semaphore_signal(barrier, inc=1, device_id=(sib, r), device_id_type=MESH)

    @pl.loop(1, 8)
    def _(d):
        pl.semaphore_signal(barrier, inc=1, device_id=(along(d), r), device_id_type=MESH)

    @pl.loop(1, 16)
    def _(i):
        p = (me + i) % 16
        pl.semaphore_signal(barrier, inc=1, device_id=(plane(p // 8), p % 8), device_id_type=MESH)

    take_w = pltpu.make_async_copy(w_in, w, in_s.at[0])
    take_w.start()
    take_cot = pltpu.make_async_copy(cot_in, cot, in_s.at[1])
    take_cot.start()
    lane = lax.broadcasted_iota(jnp.int32, (8, TILE), 1)
    for s in range(4):
        index = jnp.full((8, TILE), SLOTS, jnp.int32)
        for k in range(SLOTS):
            index = jnp.where((lane == slots[s, k]) & (k < counts[0, s]), k, index)
        inv[s] = index
    pl.semaphore_wait(barrier, 23)

    sent = []

    def later(what, sem):
        sent.append(lambda: landed(what, sem))

    def peer(i):
        return (me + i) % 16

    def fellow(i):
        return (r + jnp.where(core == 0, i, 8 - i)) % 8

    def giver(i):
        return (r + jnp.where(core == 0, 8 - i, i)) % 8

    def own(h):
        return feat.at[mine, columns_of(h)]

    def shifted(d, y):
        return jnp.where((q == 3) & (y == 0), (d + 1) % 8, d)

    def spread(h, d):
        src = own(h) if d == 0 else ring.at[h, d]
        dst = blocks.at[h, q, mine]
        if d == 0:
            y = 1 - yh
            remote(src, dst, f_s.at[h], f_r.at[h, yh * 4 + r // 2], plane(y), shifted(0, y)).start()

            @pl.when(r == 0)
            def _():
                for s in range(4):
                    rows = pl.ds(s * GROUP, GROUP)
                    pltpu.make_async_copy(
                        feat.at[rows, columns_of(h)], blocks.at[h, q, rows], f_r.at[h, yh * 4 + s]
                    ).start()

            return
        for y in range(2):
            to = shifted(d, y)
            here = (yh == y) & (r == to)

            @pl.when(here)
            def _():
                pltpu.make_async_copy(src, dst, f_r.at[h, yh * 4 + r // 2]).start()

            @pl.when(jnp.logical_not(here))
            def _():
                remote(src, dst, f_s.at[h], f_r.at[h, yh * 4 + r // 2], plane(y), to).start()

    for h in range(PARTS):
        remote(own(h), ring.at[h, 1], z_s.at[h], z_r.at[h, 1], down, r).start()
        remote(own(h), ring.at[h, 7], z_s.at[h], z_r.at[h, 7], up, r).start()
    for m in range(4):
        off = q - 2 + m
        turn = jnp.where(off < -1, -1, jnp.where(off >= 4, 1, 0))
        slot = (off + 4) % 4
        to = (r + turn + 8) % 8

        @pl.when(turn == 0)
        def _():
            pltpu.make_async_copy(tiles.at[m], tl.at[slot, pl.ds(0, SLOTS)], t_r.at[slot]).start()
            pltpu.make_async_copy(inv.at[m], invv.at[slot], i_r.at[slot]).start()

        @pl.when(turn != 0)
        def _():
            remote(tiles.at[m], tl.at[slot, pl.ds(0, SLOTS)], t_s.at[m], t_r.at[slot], b, to).start()
            remote(inv.at[m], invv.at[slot], i_s.at[m], i_r.at[slot], b, to).start()

    def forward_ring(h, k):
        landed(ring.at[h, k], z_r.at[h, k])
        landed(ring.at[h, 8 - k], z_r.at[h, 8 - k])
        if k < 3:
            remote(ring.at[h, k], ring.at[h, k + 1], z_s.at[h], z_r.at[h, k + 1], down, r).start()
            remote(ring.at[h, 8 - k], ring.at[h, 7 - k], z_s.at[h], z_r.at[h, 7 - k], up, r).start()
        else:
            remote(ring.at[h, 3, low], ring.at[h, 4, low], z_s.at[h], z_r.at[h, 4], down, r).start()
            remote(ring.at[h, 5, high], ring.at[h, 4, high], z_s.at[h], z_r.at[h, 0], up, r).start()

    def last_of_ring(h):
        landed(ring.at[h, 4, low], z_r.at[h, 4])
        landed(ring.at[h, 4, high], z_r.at[h, 0])

    for turn in range(PARTS + 4):
        for h in range(PARTS):
            k = turn - h
            if k == 0:
                spread(h, 0)
            elif 1 <= k <= 3:
                forward_ring(h, k)
                spread(h, k)
                spread(h, 8 - k)
            elif k == 4:
                last_of_ring(h)
                spread(h, 4)
    for h in range(PARTS):
        later(ring.at[h, pl.ds(0, 7)], z_s.at[h])

    def features_sent():
        for count, which in ((15, r == 0), (14, r != 0)):
            @pl.when(which)
            def _():
                for h in range(PARTS):
                    landed(heap.at[h, pl.ds(0, count)], f_s.at[h])

    sent.append(features_sent)

    def lists_sent():
        for m in range(4):
            off = q - 2 + m

            @pl.when((off < -1) | (off >= 4))
            def _():
                landed(tiles.at[m], t_s.at[m])
                landed(inv.at[m], i_s.at[m])

    sent.append(lists_sent)
    take_w.wait()
    wt[...] = w[...].T
    for s in range(4):
        landed(tl.at[s, pl.ds(0, SLOTS)], t_r.at[s])
        landed(invv.at[s], i_r.at[s])
    move = pltpu.make_async_copy(invv, invs, i_l.at[0])
    move.start()
    zero = jnp.zeros((TILE, TILE), BF16)
    for s in range(4):
        tl[s, SLOTS] = zero
        tt[s, SLOTS] = zero

    @pl.loop(0, 4 * SLOTS)
    def _(i):
        tt[i // SLOTS, i % SLOTS] = tl[i // SLOTS, i % SLOTS].T

    move.wait()

    @pl.loop(0, 4 * TILES)
    def _(i):
        s, t = i // TILES, i % TILES
        for c in range(TILES):
            dense[s, tile_rows(t), c * TILE:(c + 1) * TILE] = tl[s, invs[s, 0, t * TILES + c]]
            denset[s, tile_rows(t), c * TILE:(c + 1) * TILE] = tt[s, invs[s, 0, c * TILES + t]]

    take_cot.wait()

    def pass_on(h):
        @pl.loop(0, 8)
        def _(i):
            piece = blocks.at[h, 2 * (i // 4) + core, group_rows(i % 4)]
            landed(piece, f_r.at[h, i])
            remote(piece, piece, s_s.at[h], s_r.at[h], sib, r).start()

        later(heap.at[h], s_s.at[h])

    def own_blocks(h):
        @pl.loop(0, GROUPS)
        def _(g):
            rows = group_rows(g)
            acc[h, rows] = dot(dense[core, rows, :], blocks[h, core]) + dot(
                dense[2 + core, rows, :], blocks[h, 2 + core]
            )

    def sibling_blocks(h):
        landed(heap.at[h], s_r.at[h])

        @pl.loop(0, GROUPS)
        def _(i):
            g = (r // 2 + jnp.where(core == 0, 1 + i, 3 - i)) % GROUPS
            rows = group_rows(g)
            value = dot(dense[1 - core, rows, :], blocks[h, 1 - core]) + dot(
                dense[3 - core, rows, :], blocks[h, 3 - core]
            )
            part[h, rows] = (acc[h, rows] + value).astype(BF16)
            for j in range(2):
                t = 2 * g + j

                @pl.when(t != r)
                def _():
                    remote(part.at[h, tile_rows(t)], parts.at[h, r], p_s.at[h], p_r.at[h], b, t).start()

        later(parts.at[h, pl.ds(0, 7)], p_s.at[h])

    def add_parts(h):
        landed(parts.at[h, pl.ds(0, 7)], p_r.at[h])
        acc[h, 0:TILE] = part[h, mine].astype(F32)

        @pl.loop(1, 8)
        def _(i):
            acc[h, 0:TILE] += parts[h, giver(i)].astype(F32)

        agg[h, mine] = acc[h, 0:TILE].astype(BF16)

    def share(h):
        @pl.loop(1, 8)
        def _(i):
            t = fellow(i)
            remote(agg.at[h, mine], agg.at[h, mine], a_s.at[h], a_r.at[r], b, t).start()

        later(parts.at[h, pl.ds(0, 7)], a_s.at[h])

    for h in range(PARTS):
        pass_on(h)
        own_blocks(h)
        sibling_blocks(h)
        if h >= 2:
            add_parts(h - 2)
            share(h - 2)
    for h in range(PARTS - 2, PARTS):
        add_parts(h)
        share(h)

    def chunk(c):
        rows = tile_rows(c)
        inputs = jnp.concatenate([agg[h, rows] for h in range(PARTS)], axis=1)
        pre = dot(inputs, w[...])
        square = pre * pre
        t = jnp.tanh(K0 * (pre + K1 * square * pre))
        half = 0.5 * (1.0 + t)
        act[rows] = (pre * half).astype(BF16)
        pltpu.make_async_copy(act.at[rows], act_out.at[rows], out_s.at[0]).start()
        slope = half + 0.5 * pre * (1.0 - t * t) * (K0 * (1.0 + 3.0 * K1 * square))
        delta = (cot[rows].astype(F32) * slope).astype(BF16)
        value = dot(delta, wt[...]).astype(BF16)
        for h in range(PARTS):
            back[h, rows] = value[:, h * WIDTH:(h + 1) * WIDTH]
        return inputs, delta

    gw_part[...] = lax.dot_general(
        *chunk(r), (((0,), (0,)), ((), ())), preferred_element_type=F32
    )
    gw_send[...] = gw_part[group_rows(1 - core)].astype(BF16)
    remote(gw_send, gw_recv, wx_s.at[0], wx_r.at[0], sib, r).start()
    later(gw_send, wx_s.at[0])

    @pl.loop(1, 8)
    def _(i):
        c = giver(i)
        landed(agg.at[0, pl.ds(0, PARTS * TILE)], a_r.at[c])
        chunk(c)

    landed(gw_recv, wx_r.at[0])
    gw_half[...] = (gw_part[group_rows(core)] + gw_recv[...].astype(F32)).astype(BF16)

    @pl.loop(1, 16)
    def _(i):
        p = (me + i) % 16
        remote(
            gw_half.at[part_rows(p)], gw_quarter.at[part_rows(me)], wq_s.at[0], wq_r.at[0],
            plane(p // 8), p % 8,
        ).start()

    later(gw_half.at[pl.ds(0, 240)], wq_s.at[0])
    def side_by_side(ref, pair, *at):
        return jnp.concatenate([ref[(2 * pair, *at)], ref[(2 * pair + 1, *at)]], axis=1)

    def sibling_grads(pair):
        @pl.loop(0, 2 * GROUPS)
        def _(i):
            y, g = i // GROUPS, i % GROUPS
            rows = group_rows(g)
            value = dot(denset[2 * y + 1 - core, rows, :], side_by_side(back, pair)).astype(BF16)
            for n in range(2):
                h = 2 * pair + n
                sib_out[h, y, rows] = value[:, n * WIDTH:(n + 1) * WIDTH]
                remote(
                    sib_out.at[h, y, rows], sib_in.at[h, y, rows], b_s.at[h], b_r.at[h], sib, r
                ).start()

        for n in range(2):
            later(sib_out.at[2 * pair + n], b_s.at[2 * pair + n])

    def own_grads(pair):
        for n in range(2):
            landed(sib_in.at[2 * pair + n], b_r.at[2 * pair + n])

        @pl.loop(0, 2 * GROUPS)
        def _(i):
            j = i % 4
            y, g = (i + i // 4) % 2, (r // 2 + 2 * j + 1 + 5 * (j // 2)) % GROUPS
            rows = group_rows(g)
            value = dot(denset[2 * y + core, rows, :], side_by_side(back, pair))
            turned = jnp.where((yh == 0) & (core == 1) & (y == 1), (r + 7) % 8, r)
            for n in range(2):
                h = 2 * pair + n
                own_out[h, y, rows] = (
                    value[:, n * WIDTH:(n + 1) * WIDTH] + sib_in[h, y, rows].astype(F32)
                ).astype(BF16)
                for j in range(2):
                    t = 2 * g + j
                    src, dst = own_out.at[h, y, tile_rows(t)], heap.at[h, me]
                    here = (yh == y) & (r == t)

                    @pl.when(here)
                    def _():
                        pltpu.make_async_copy(src, dst, o_r.at[h, turned]).start()

                    @pl.when(jnp.logical_not(here))
                    def _():
                        remote(src, dst, o_s.at[h], o_r.at[h, turned], plane(y), t).start()

        for n in range(2):
            later(heap.at[0, pl.ds(0, 15)], o_s.at[2 * pair + n])

    sibling_grads(0)
    sibling_grads(1)
    own_grads(0)
    own_grads(1)
    landed(gw_quarter.at[pl.ds(0, 240)], wq_r.at[0])
    gw_ring[0] = gw_half[part_rows(me)].astype(F32)

    @pl.loop(1, 16)
    def _(i):
        p = (me + i) % 16
        gw_ring[0] += gw_quarter[part_rows(p)].astype(F32)

    @pl.loop(1, 8)
    def _(d):
        remote(gw_ring.at[0], gw_ring.at[d], wz_s.at[0], wz_r.at[0], along(d), r).start()

    later(gw_ring.at[pl.ds(0, 7)], wz_s.at[0])

    def send_along(h):
        @pl.loop(0, 8)
        def _(i):
            d = 2 * ((r // 2 + 7 - i // 2 - 2 * yh) % 4) + i % 2
            first = shifted(d, 0)
            landed(heap.at[h, pl.ds(0, 2)], o_r.at[h, d])
            value = heap[h, first].astype(F32) + heap[h, 8 + d].astype(F32)

            @pl.when(d == 0)
            def _():
                total[h] = value

            @pl.when(d != 0)
            def _():
                hop_out[h, d] = value.astype(BF16)
                remote(hop_out.at[h, d], hop_in.at[h, d], h_s.at[h], h_r.at[h], along(d), r).start()

        later(ring.at[h, pl.ds(0, 7)], h_s.at[h])

    def finish(h):
        landed(hop_in.at[h, pl.ds(0, 7)], h_r.at[h])

        @pl.loop(1, 8)
        def _(d):
            total[h] += hop_in[h, d].astype(F32)

        place = grad.at[h, mine]
        grad[h, mine] = total[h].astype(BF16)

        @pl.loop(1, 8)
        def _(i):
            t = fellow(i)
            remote(place, place, g_s.at[h], g_r.at[h], b, t).start()

        later(parts.at[h, pl.ds(0, 7)], g_s.at[h])

    send_along(0)
    send_along(1)
    landed(gw_ring.at[pl.ds(0, 7)], wz_r.at[0])

    whole = gw_ring[z]
    for k in range(1, 8):
        whole = whole + gw_ring[(z + 8 - k) % 8]
    place = pl.ds(pl.multiple_of(core * 256 + me * 16, 16), 16)
    gw_fin[place] = (whole * (1.0 / math.sqrt(32 * ROWS))).astype(BF16)

    @pl.loop(1, 16)
    def _(i):
        p = (me + i) % 16
        remote(
            gw_fin.at[place], gw_fin.at[place], wf_s.at[0], wf_r.at[0], plane(p // 8), p % 8
        ).start()

    later(gw_half.at[pl.ds(0, 240)], wf_s.at[0])

    for h in range(PARTS):
        finish(h)
        if h + 2 < PARTS:
            send_along(h + 2)

    landed(gw_fin.at[pl.ds(0, 240)], wf_r.at[0])
    landed(act, out_s.at[0])

    half = group_rows(core)
    remote(gw_fin.at[half], gw_fin.at[half], wy_s.at[0], wy_r.at[0], sib, r).start()
    later(gw_fin.at[half], wy_s.at[0])
    landed(gw_fin.at[group_rows(1 - core)], wy_r.at[0])
    give_gw = pltpu.make_async_copy(gw_fin, gw, in_s.at[0])
    give_gw.start()

    for h in range(PARTS):
        landed(parts.at[h, pl.ds(0, 7)], g_r.at[h])
        pltpu.make_async_copy(grad.at[h], gin.at[:, columns_of(h)], out_s.at[h]).start()

    for wait in sent:
        wait()
    give_gw.wait()
    for h in range(PARTS):
        landed(grad.at[h], out_s.at[h])


def hand_over_kernel(act, grad, weight, act_out, grad_out, weight_out, held, narrow, wide, get, give):
    rows = ROWS // 4
    gets, gives = [], []
    for n, (src, dst) in enumerate(((act, act_out), (grad, grad_out))):
        for m in range(4):
            part, place = pl.ds(m * rows, rows), held.at[4 * n + m]
            gets.append(pltpu.make_async_copy(src.at[part], place, get.at[4 * n + m]))
            gives.append(pltpu.make_async_copy(place, dst.at[part], give.at[4 * n + m]))
    take = pltpu.make_async_copy(weight, narrow, get.at[8])
    take.start()
    for copy in gets:
        copy.start()
    take.wait()
    wide[...] = narrow[...].astype(F32)
    put = pltpu.make_async_copy(wide, weight_out, give.at[8])
    put.start()
    for first, second in zip(gets, gives):
        first.wait()
        second.start()
    for copy in gives:
        copy.wait()
    put.wait()


def hand_over(act, grad, weight):
    hbm = pl.BlockSpec(memory_space=pl.ANY)
    return pl.pallas_call(
        hand_over_kernel,
        out_shape=(
            jax.ShapeDtypeStruct((ROWS, FEATURES), BF16),
            jax.ShapeDtypeStruct((ROWS, FEATURES), BF16),
            jax.ShapeDtypeStruct((FEATURES, FEATURES), F32),
        ),
        in_specs=[hbm, hbm, hbm],
        out_specs=(hbm, hbm, hbm),
        scratch_shapes=[
            pltpu.VMEM((8, ROWS // 4, FEATURES), BF16),
            pltpu.VMEM((FEATURES, FEATURES), BF16),
            pltpu.VMEM((FEATURES, FEATURES), F32),
            pltpu.SemaphoreType.DMA((9,)),
            pltpu.SemaphoreType.DMA((9,)),
        ],
        compiler_params=pltpu.CompilerParams(vmem_limit_bytes=60 * 1024 * 1024),
        cost_estimate=pl.CostEstimate(flops=0, bytes_accessed=6 << 20, transcendentals=0),
    )(act, grad, weight)


def per_device(features, layer_weight, adjacency_tiles, tile_slots, tile_counts, cotangent):
    hbm = pl.BlockSpec(memory_space=pl.ANY)
    smem = pl.BlockSpec(memory_space=pltpu.SMEM)
    dma = pltpu.SemaphoreType.DMA
    half = (PARTS, ROWS, WIDTH)
    slices = (PARTS, 8, TILE, WIDTH)
    scratch = [
        pltpu.VMEM((FEATURES, FEATURES), BF16),
        pltpu.VMEM((FEATURES, FEATURES), BF16),
        pltpu.VMEM((ROWS, FEATURES), BF16),
        pltpu.VMEM((ROWS, FEATURES), BF16),
        pltpu.VMEM((4, SLOTS + 1, TILE, TILE), BF16),
        pltpu.VMEM((4, SLOTS + 1, TILE, TILE), BF16),
        pltpu.VMEM((4, 8, TILE), jnp.int32),
        pltpu.VMEM((4, 8, TILE), jnp.int32),
        pltpu.SMEM((4, 8, TILE), jnp.int32),
        pltpu.VMEM((4, ROWS, ROWS), BF16),
        pltpu.VMEM((4, ROWS, ROWS), BF16),
        pltpu.VMEM(slices, BF16),
        pltpu.VMEM((PARTS, 4, ROWS, WIDTH), BF16),
        pltpu.VMEM(half, F32),
        pltpu.VMEM(half, BF16),
        pltpu.VMEM(slices, BF16),
        pltpu.VMEM(half, BF16),
        pltpu.VMEM(half, BF16),
        pltpu.VMEM((PARTS, 2, ROWS, WIDTH), BF16),
        pltpu.VMEM((PARTS, 2, ROWS, WIDTH), BF16),
        pltpu.VMEM((PARTS, 2, ROWS, WIDTH), BF16),
        pltpu.VMEM((PARTS, 16, TILE, WIDTH), BF16),
        pltpu.VMEM((PARTS, TILE, WIDTH), F32),
        pltpu.VMEM(slices, BF16),
        pltpu.VMEM(slices, BF16),
        pltpu.VMEM(half, BF16),
        pltpu.VMEM((FEATURES, FEATURES), F32),
        pltpu.VMEM((256, FEATURES), BF16),
        pltpu.VMEM((256, FEATURES), BF16),
        pltpu.VMEM((256, FEATURES), BF16),
        pltpu.VMEM((256, FEATURES), BF16),
        pltpu.VMEM((8, 16, FEATURES), F32),
        pltpu.VMEM((FEATURES, FEATURES), BF16),
    ]
    two = PARTS
    two = (PARTS,)
    sems = [
        (2,), (PARTS,),
        (4,), (4,), (4,), (4,), (1,),
        two, (PARTS, 8), two, (PARTS, 8), two, two,
        two, two, two, (8,),
        two, two, two, (PARTS, 8), two, two, two, two,
        (1,), (1,), (1,), (1,), (1,), (1,), (1,), (1,), (1,), (1,),
    ]
    activated, grad_input, grad_weight = pl.pallas_call(
        kernel,
        out_shape=(
            jax.ShapeDtypeStruct((ROWS, FEATURES), BF16),
            jax.ShapeDtypeStruct((ROWS, FEATURES), BF16),
            jax.ShapeDtypeStruct((FEATURES, FEATURES), BF16),
        ),
        in_specs=[hbm, hbm, hbm, smem, smem, hbm],
        out_specs=(hbm, hbm, hbm),
        scratch_shapes=scratch + [dma(n) for n in sems],
        compiler_params=pltpu.CompilerParams(
            collective_id=0, has_side_effects=True, vmem_limit_bytes=58 * 1024 * 1024
        ),
        cost_estimate=pl.CostEstimate(
            flops=10 * 2 * ROWS * ROWS * FEATURES, bytes_accessed=8 << 20, transcendentals=ROWS * FEATURES
        ),
    )(features, layer_weight, adjacency_tiles[0], tile_slots[0], tile_counts, cotangent)
    return hand_over(activated, grad_input, grad_weight)


def solution(mesh):
    return jax.shard_map(
        per_device,
        mesh=mesh,
        in_specs=(
            P("blk", None),
            P(),
            P("blk", "rep", None, None, None),
            P("blk", "rep", None),
            P("blk", "rep"),
            P("blk", None),
        ),
        out_specs=(P("blk", None), P("blk", None), P()),
        check_vma=False,
    )
```

```python
import math

import jax
import jax.numpy as jnp
from jax import lax
from jax.experimental import pallas as pl
from jax.experimental.pallas import tpu as pltpu
from jax.sharding import PartitionSpec as P

MESH = pl.DeviceIdType.MESH
F32, BF16 = jnp.float32, jnp.bfloat16
FEATURES = 512
TILE = 128
TILES = 8
SLOTS = 8
ROWS = 1024
GROUP = 256
GROUPS = ROWS // GROUP
PARTS = 4
WIDTH = FEATURES // PARTS
K0 = math.sqrt(2.0 / math.pi)
K1 = 0.044715


def tile_rows(t):
    return pl.ds(pl.multiple_of(t * TILE, TILE), TILE)


def group_rows(g):
    return pl.ds(pl.multiple_of(g * GROUP, GROUP), GROUP)


def part_rows(p):
    return pl.ds(pl.multiple_of(p * 16, 16), 16)


def columns_of(h):
    return pl.ds(h * WIDTH, WIDTH)


def remote(src, dst, send, recv, blk, rep):
    return pltpu.make_async_remote_copy(
        src_ref=src, dst_ref=dst, send_sem=send, recv_sem=recv,
        device_id=(blk, rep), device_id_type=MESH,
    )


def landed(dst, sem):
    pltpu.make_async_copy(dst, dst, sem).wait()


def dot(a, b):
    return jnp.dot(a, b, preferred_element_type=F32)


def kernel(
    feat, w_in, tiles, slots, counts, cot_in, act_out, gin, gw,
    w, wt, cot, act, tl, tt, inv, invv, invs, dense, denset, ring, blocks, acc, part, parts, agg, back,
    sib_out, sib_in, own_out, heap, total, hop_out, hop_in, grad,
    gw_part, gw_send, gw_recv, gw_half, gw_quarter, gw_ring, gw_fin,
    in_s, out_s,
    t_s, t_r, i_s, i_r, i_l, z_s, z_r, f_s, f_r, s_s, s_r, p_s, p_r, a_s, a_r,
    b_s, b_r, o_s, o_r, h_s, h_r, g_s, g_r,
    wx_s, wx_r, wq_s, wq_r, wz_s, wz_r, wf_s, wf_r, wy_s, wy_r,
):
    b = lax.axis_index("blk")
    r = lax.axis_index("rep")
    z, q = b // 4, b % 4
    yh, core = q // 2, q % 2
    me = yh * 8 + r
    sib = b + 1 - 2 * core
    up = ((z + 1) % 8) * 4 + q
    down = ((z + 7) % 8) * 4 + q
    mine = tile_rows(r)
    low, high = pl.ds(0, TILE // 2), pl.ds(TILE // 2, TILE // 2)

    def plane(y):
        return 4 * z + 2 * y + core

    def along(d):
        return ((z + d) % 8) * 4 + q

    barrier = pltpu.get_barrier_semaphore()
    pl.semaphore_signal(barrier, inc=1, device_id=(sib, r), device_id_type=MESH)

    @pl.loop(1, 8)
    def _(d):
        pl.semaphore_signal(barrier, inc=1, device_id=(along(d), r), device_id_type=MESH)

    @pl.loop(1, 16)
    def _(i):
        p = (me + i) % 16
        pl.semaphore_signal(barrier, inc=1, device_id=(plane(p // 8), p % 8), device_id_type=MESH)

    take_w = pltpu.make_async_copy(w_in, w, in_s.at[0])
    take_w.start()
    take_cot = pltpu.make_async_copy(cot_in, cot, in_s.at[1])
    take_cot.start()
    lane = lax.broadcasted_iota(jnp.int32, (8, TILE), 1)
    for s in range(4):
        index = jnp.full((8, TILE), SLOTS, jnp.int32)
        for k in range(SLOTS):
            index = jnp.where((lane == slots[s, k]) & (k < counts[0, s]), k, index)
        inv[s] = index
    pl.semaphore_wait(barrier, 23)

    sent = []

    def later(what, sem):
        sent.append(lambda: landed(what, sem))

    def peer(i):
        return (me + i) % 16

    def fellow(i):
        return (r + jnp.where(core == 0, i, 8 - i)) % 8

    def giver(i):
        return (r + jnp.where(core == 0, 8 - i, i)) % 8

    def own(h):
        return feat.at[mine, columns_of(h)]

    def shifted(d, y):
        return jnp.where((q == 3) & (y == 0), (d + 1) % 8, d)

    def spread(h, d):
        src = own(h) if d == 0 else ring.at[h, d]
        dst = blocks.at[h, q, mine]
        if d == 0:
            y = 1 - yh
            remote(src, dst, f_s.at[h], f_r.at[h, yh], plane(y), shifted(0, y)).start()

            @pl.when(r == 0)
            def _():
                pltpu.make_async_copy(
                    feat.at[:, columns_of(h)], blocks.at[h, q], f_r.at[h, yh]
                ).start()

            return
        for y in range(2):
            to = shifted(d, y)
            here = (yh == y) & (r == to)

            @pl.when(here)
            def _():
                pltpu.make_async_copy(src, dst, f_r.at[h, yh]).start()

            @pl.when(jnp.logical_not(here))
            def _():
                remote(src, dst, f_s.at[h], f_r.at[h, yh], plane(y), to).start()

    for h in range(PARTS):
        remote(own(h), ring.at[h, 1], z_s.at[h], z_r.at[h, 1], down, r).start()
        remote(own(h), ring.at[h, 7], z_s.at[h], z_r.at[h, 7], up, r).start()
    for m in range(4):
        off = q - 2 + m
        turn = jnp.where(off < -1, -1, jnp.where(off >= 4, 1, 0))
        slot = (off + 4) % 4
        to = (r + turn + 8) % 8

        @pl.when(turn == 0)
        def _():
            pltpu.make_async_copy(tiles.at[m], tl.at[slot, pl.ds(0, SLOTS)], t_r.at[slot]).start()
            pltpu.make_async_copy(inv.at[m], invv.at[slot], i_r.at[slot]).start()

        @pl.when(turn != 0)
        def _():
            remote(tiles.at[m], tl.at[slot, pl.ds(0, SLOTS)], t_s.at[m], t_r.at[slot], b, to).start()
            remote(inv.at[m], invv.at[slot], i_s.at[m], i_r.at[slot], b, to).start()

    def forward_ring(h, k):
        landed(ring.at[h, k], z_r.at[h, k])
        landed(ring.at[h, 8 - k], z_r.at[h, 8 - k])
        if k < 3:
            remote(ring.at[h, k], ring.at[h, k + 1], z_s.at[h], z_r.at[h, k + 1], down, r).start()
            remote(ring.at[h, 8 - k], ring.at[h, 7 - k], z_s.at[h], z_r.at[h, 7 - k], up, r).start()
        else:
            remote(ring.at[h, 3, low], ring.at[h, 4, low], z_s.at[h], z_r.at[h, 4], down, r).start()
            remote(ring.at[h, 5, high], ring.at[h, 4, high], z_s.at[h], z_r.at[h, 0], up, r).start()

    def last_of_ring(h):
        landed(ring.at[h, 4, low], z_r.at[h, 4])
        landed(ring.at[h, 4, high], z_r.at[h, 0])

    for turn in range(PARTS + 4):
        for h in range(PARTS):
            k = turn - h
            if k == 0:
                spread(h, 0)
            elif 1 <= k <= 3:
                forward_ring(h, k)
                spread(h, k)
                spread(h, 8 - k)
            elif k == 4:
                last_of_ring(h)
                spread(h, 4)
    for h in range(PARTS):
        later(ring.at[h, pl.ds(0, 7)], z_s.at[h])

    def features_sent():
        for count, which in ((15, r == 0), (14, r != 0)):
            @pl.when(which)
            def _():
                for h in range(PARTS):
                    landed(heap.at[h, pl.ds(0, count)], f_s.at[h])

    sent.append(features_sent)

    def lists_sent():
        for m in range(4):
            off = q - 2 + m

            @pl.when((off < -1) | (off >= 4))
            def _():
                landed(tiles.at[m], t_s.at[m])
                landed(inv.at[m], i_s.at[m])

    sent.append(lists_sent)
    take_w.wait()
    wt[...] = w[...].T
    for s in range(4):
        landed(tl.at[s, pl.ds(0, SLOTS)], t_r.at[s])
        landed(invv.at[s], i_r.at[s])
    move = pltpu.make_async_copy(invv, invs, i_l.at[0])
    move.start()
    zero = jnp.zeros((TILE, TILE), BF16)
    for s in range(4):
        tl[s, SLOTS] = zero
        tt[s, SLOTS] = zero

    move.wait()

    @pl.loop(0, 4 * TILES)
    def _(i):
        s, t = i // TILES, i % TILES
        for c in range(TILES):
            dense[s, tile_rows(t), c * TILE:(c + 1) * TILE] = tl[s, invs[s, 0, t * TILES + c]]

    def transpose_list(s):
        @pl.loop(0, SLOTS)
        def _(i):
            tt[s, i] = tl[s, i].T

        @pl.loop(0, TILES)
        def _(t):
            for c in range(TILES):
                denset[s, tile_rows(t), c * TILE:(c + 1) * TILE] = tt[s, invs[s, 0, c * TILES + t]]

    take_cot.wait()

    def pass_on(h):
        for y in range(2):
            piece = blocks.at[h, 2 * y + core]
            landed(piece, f_r.at[h, y])
            remote(piece, piece, s_s.at[h], s_r.at[h], sib, r).start()

        later(heap.at[h], s_s.at[h])

    def own_blocks(h):
        @pl.loop(0, GROUPS)
        def _(g):
            rows = group_rows(g)
            acc[h, rows] = dot(dense[core, rows, :], blocks[h, core]) + dot(
                dense[2 + core, rows, :], blocks[h, 2 + core]
            )

    def sibling_blocks(h):
        landed(heap.at[h], s_r.at[h])

        @pl.loop(0, GROUPS)
        def _(i):
            g = (r // 2 + jnp.where(core == 0, 1 + i, 3 - i)) % GROUPS
            rows = group_rows(g)
            value = dot(dense[1 - core, rows, :], blocks[h, 1 - core]) + dot(
                dense[3 - core, rows, :], blocks[h, 3 - core]
            )
            part[h, rows] = (acc[h, rows] + value).astype(BF16)
            for j in range(2):
                t = 2 * g + j

                @pl.when(t != r)
                def _():
                    remote(part.at[h, tile_rows(t)], parts.at[h, r], p_s.at[h], p_r.at[h], b, t).start()

        later(parts.at[h, pl.ds(0, 7)], p_s.at[h])

    def add_parts(h):
        landed(parts.at[h, pl.ds(0, 7)], p_r.at[h])
        acc[h, 0:TILE] = part[h, mine].astype(F32)

        @pl.loop(1, 8)
        def _(i):
            acc[h, 0:TILE] += parts[h, giver(i)].astype(F32)

        agg[h, mine] = acc[h, 0:TILE].astype(BF16)

    def share(h):
        @pl.loop(1, 8)
        def _(i):
            t = fellow(i)
            remote(agg.at[h, mine], agg.at[h, mine], a_s.at[h], a_r.at[r], b, t).start()

        later(parts.at[h, pl.ds(0, 7)], a_s.at[h])

    for h in range(PARTS):
        if h > 0:
            transpose_list(h - 1)
        pass_on(h)
        own_blocks(h)
        sibling_blocks(h)
        if h >= 2:
            add_parts(h - 2)
            share(h - 2)
    for h in range(PARTS - 2, PARTS):
        add_parts(h)
        share(h)
    transpose_list(3)

    def chunk(c):
        rows = tile_rows(c)
        inputs = jnp.concatenate([agg[h, rows] for h in range(PARTS)], axis=1)
        pre = dot(inputs, w[...])
        square = pre * pre
        t = jnp.tanh(K0 * (pre + K1 * square * pre))
        half = 0.5 * (1.0 + t)
        act[rows] = (pre * half).astype(BF16)
        pltpu.make_async_copy(act.at[rows], act_out.at[rows], out_s.at[0]).start()
        slope = half + 0.5 * pre * (1.0 - t * t) * (K0 * (1.0 + 3.0 * K1 * square))
        delta = (cot[rows].astype(F32) * slope).astype(BF16)
        value = dot(delta, wt[...]).astype(BF16)
        for h in range(PARTS):
            back[h, rows] = value[:, h * WIDTH:(h + 1) * WIDTH]
        return inputs, delta

    gw_part[...] = lax.dot_general(
        *chunk(r), (((0,), (0,)), ((), ())), preferred_element_type=F32
    )
    gw_send[...] = gw_part[group_rows(1 - core)].astype(BF16)
    remote(gw_send, gw_recv, wx_s.at[0], wx_r.at[0], sib, r).start()
    later(gw_send, wx_s.at[0])

    @pl.loop(1, 8)
    def _(i):
        c = giver(i)
        landed(agg.at[0, pl.ds(0, PARTS * TILE)], a_r.at[c])
        chunk(c)

    landed(gw_recv, wx_r.at[0])
    gw_half[...] = (gw_part[group_rows(core)] + gw_recv[...].astype(F32)).astype(BF16)

    @pl.loop(1, 16)
    def _(i):
        p = (me + i) % 16
        remote(
            gw_half.at[part_rows(p)], gw_quarter.at[part_rows(me)], wq_s.at[0], wq_r.at[0],
            plane(p // 8), p % 8,
        ).start()

    later(gw_half.at[pl.ds(0, 240)], wq_s.at[0])
    def side_by_side(ref, pair, *at):
        return jnp.concatenate([ref[(2 * pair, *at)], ref[(2 * pair + 1, *at)]], axis=1)

    def sibling_grads(pair):
        @pl.loop(0, 2 * GROUPS)
        def _(i):
            y, g = i // GROUPS, i % GROUPS
            rows = group_rows(g)
            value = dot(denset[2 * y + 1 - core, rows, :], side_by_side(back, pair)).astype(BF16)
            for n in range(2):
                h = 2 * pair + n
                sib_out[h, y, rows] = value[:, n * WIDTH:(n + 1) * WIDTH]
                remote(
                    sib_out.at[h, y, rows], sib_in.at[h, y, rows], b_s.at[h], b_r.at[h], sib, r
                ).start()

        for n in range(2):
            later(sib_out.at[2 * pair + n], b_s.at[2 * pair + n])

    def own_grads(pair):
        for n in range(2):
            landed(sib_in.at[2 * pair + n], b_r.at[2 * pair + n])

        @pl.loop(0, 2 * GROUPS)
        def _(i):
            j = i % 4
            y, g = (i + i // 4) % 2, (r // 2 + 2 * j + 1 + 5 * (j // 2)) % GROUPS
            rows = group_rows(g)
            value = dot(denset[2 * y + core, rows, :], side_by_side(back, pair))
            turned = jnp.where((yh == 0) & (core == 1) & (y == 1), (r + 7) % 8, r)
            for n in range(2):
                h = 2 * pair + n
                own_out[h, y, rows] = (
                    value[:, n * WIDTH:(n + 1) * WIDTH] + sib_in[h, y, rows].astype(F32)
                ).astype(BF16)
                for j in range(2):
                    t = 2 * g + j
                    src, dst = own_out.at[h, y, tile_rows(t)], heap.at[h, me]
                    here = (yh == y) & (r == t)

                    @pl.when(here)
                    def _():
                        pltpu.make_async_copy(src, dst, o_r.at[h, turned]).start()

                    @pl.when(jnp.logical_not(here))
                    def _():
                        remote(src, dst, o_s.at[h], o_r.at[h, turned], plane(y), t).start()

        for n in range(2):
            later(heap.at[0, pl.ds(0, 15)], o_s.at[2 * pair + n])

    sibling_grads(0)
    sibling_grads(1)
    own_grads(0)
    own_grads(1)
    landed(gw_quarter.at[pl.ds(0, 240)], wq_r.at[0])
    gw_ring[0] = gw_half[part_rows(me)].astype(F32)

    @pl.loop(1, 16)
    def _(i):
        p = (me + i) % 16
        gw_ring[0] += gw_quarter[part_rows(p)].astype(F32)

    @pl.loop(1, 8)
    def _(d):
        remote(gw_ring.at[0], gw_ring.at[d], wz_s.at[0], wz_r.at[0], along(d), r).start()

    later(gw_ring.at[pl.ds(0, 7)], wz_s.at[0])

    def send_along(h):
        @pl.loop(0, 8)
        def _(i):
            d = 2 * ((r // 2 + 7 - i // 2 - 2 * yh) % 4) + i % 2
            first = shifted(d, 0)
            landed(heap.at[h, pl.ds(0, 2)], o_r.at[h, d])
            value = heap[h, first].astype(F32) + heap[h, 8 + d].astype(F32)

            @pl.when(d == 0)
            def _():
                total[h] = value

            @pl.when(d != 0)
            def _():
                hop_out[h, d] = value.astype(BF16)
                remote(hop_out.at[h, d], hop_in.at[h, d], h_s.at[h], h_r.at[h], along(d), r).start()

        later(ring.at[h, pl.ds(0, 7)], h_s.at[h])

    def finish(h):
        landed(hop_in.at[h, pl.ds(0, 7)], h_r.at[h])

        @pl.loop(1, 8)
        def _(d):
            total[h] += hop_in[h, d].astype(F32)

        place = grad.at[h, mine]
        grad[h, mine] = total[h].astype(BF16)

        @pl.loop(1, 8)
        def _(i):
            t = fellow(i)
            remote(place, place, g_s.at[h], g_r.at[h], b, t).start()

        later(parts.at[h, pl.ds(0, 7)], g_s.at[h])

    send_along(0)
    send_along(1)
    landed(gw_ring.at[pl.ds(0, 7)], wz_r.at[0])

    whole = gw_ring[z]
    for k in range(1, 8):
        whole = whole + gw_ring[(z + 8 - k) % 8]
    place = pl.ds(pl.multiple_of(core * 256 + me * 16, 16), 16)
    gw_fin[place] = (whole * (1.0 / math.sqrt(32 * ROWS))).astype(BF16)

    @pl.loop(1, 16)
    def _(i):
        p = (me + i) % 16
        remote(
            gw_fin.at[place], gw_fin.at[place], wf_s.at[0], wf_r.at[0], plane(p // 8), p % 8
        ).start()

    later(gw_half.at[pl.ds(0, 240)], wf_s.at[0])

    for h in range(PARTS):
        finish(h)
        if h + 2 < PARTS:
            send_along(h + 2)

    landed(gw_fin.at[pl.ds(0, 240)], wf_r.at[0])
    landed(act, out_s.at[0])

    half = group_rows(core)
    remote(gw_fin.at[half], gw_fin.at[half], wy_s.at[0], wy_r.at[0], sib, r).start()
    later(gw_fin.at[half], wy_s.at[0])
    landed(gw_fin.at[group_rows(1 - core)], wy_r.at[0])
    give_gw = pltpu.make_async_copy(gw_fin, gw, in_s.at[0])
    give_gw.start()

    for h in range(PARTS):
        landed(parts.at[h, pl.ds(0, 7)], g_r.at[h])
        pltpu.make_async_copy(grad.at[h], gin.at[:, columns_of(h)], out_s.at[h]).start()

    for wait in sent:
        wait()
    give_gw.wait()
    for h in range(PARTS):
        landed(grad.at[h], out_s.at[h])


def hand_over_kernel(act, grad, weight, act_out, grad_out, weight_out, held, narrow, wide, get, give):
    rows = ROWS // 4
    gets, gives = [], []
    for n, (src, dst) in enumerate(((act, act_out), (grad, grad_out))):
        for m in range(4):
            part, place = pl.ds(m * rows, rows), held.at[4 * n + m]
            gets.append(pltpu.make_async_copy(src.at[part], place, get.at[4 * n + m]))
            gives.append(pltpu.make_async_copy(place, dst.at[part], give.at[4 * n + m]))
    take = pltpu.make_async_copy(weight, narrow, get.at[8])
    take.start()
    for copy in gets:
        copy.start()
    take.wait()
    wide[...] = narrow[...].astype(F32)
    put = pltpu.make_async_copy(wide, weight_out, give.at[8])
    put.start()
    for first, second in zip(gets, gives):
        first.wait()
        second.start()
    for copy in gives:
        copy.wait()
    put.wait()


def hand_over(act, grad, weight):
    hbm = pl.BlockSpec(memory_space=pl.ANY)
    return pl.pallas_call(
        hand_over_kernel,
        out_shape=(
            jax.ShapeDtypeStruct((ROWS, FEATURES), BF16),
            jax.ShapeDtypeStruct((ROWS, FEATURES), BF16),
            jax.ShapeDtypeStruct((FEATURES, FEATURES), F32),
        ),
        in_specs=[hbm, hbm, hbm],
        out_specs=(hbm, hbm, hbm),
        scratch_shapes=[
            pltpu.VMEM((8, ROWS // 4, FEATURES), BF16),
            pltpu.VMEM((FEATURES, FEATURES), BF16),
            pltpu.VMEM((FEATURES, FEATURES), F32),
            pltpu.SemaphoreType.DMA((9,)),
            pltpu.SemaphoreType.DMA((9,)),
        ],
        compiler_params=pltpu.CompilerParams(vmem_limit_bytes=60 * 1024 * 1024),
        cost_estimate=pl.CostEstimate(flops=0, bytes_accessed=6 << 20, transcendentals=0),
    )(act, grad, weight)


def per_device(features, layer_weight, adjacency_tiles, tile_slots, tile_counts, cotangent):
    hbm = pl.BlockSpec(memory_space=pl.ANY)
    smem = pl.BlockSpec(memory_space=pltpu.SMEM)
    dma = pltpu.SemaphoreType.DMA
    half = (PARTS, ROWS, WIDTH)
    slices = (PARTS, 8, TILE, WIDTH)
    scratch = [
        pltpu.VMEM((FEATURES, FEATURES), BF16),
        pltpu.VMEM((FEATURES, FEATURES), BF16),
        pltpu.VMEM((ROWS, FEATURES), BF16),
        pltpu.VMEM((ROWS, FEATURES), BF16),
        pltpu.VMEM((4, SLOTS + 1, TILE, TILE), BF16),
        pltpu.VMEM((4, SLOTS + 1, TILE, TILE), BF16),
        pltpu.VMEM((4, 8, TILE), jnp.int32),
        pltpu.VMEM((4, 8, TILE), jnp.int32),
        pltpu.SMEM((4, 8, TILE), jnp.int32),
        pltpu.VMEM((4, ROWS, ROWS), BF16),
        pltpu.VMEM((4, ROWS, ROWS), BF16),
        pltpu.VMEM(slices, BF16),
        pltpu.VMEM((PARTS, 4, ROWS, WIDTH), BF16),
        pltpu.VMEM(half, F32),
        pltpu.VMEM(half, BF16),
        pltpu.VMEM(slices, BF16),
        pltpu.VMEM(half, BF16),
        pltpu.VMEM(half, BF16),
        pltpu.VMEM((PARTS, 2, ROWS, WIDTH), BF16),
        pltpu.VMEM((PARTS, 2, ROWS, WIDTH), BF16),
        pltpu.VMEM((PARTS, 2, ROWS, WIDTH), BF16),
        pltpu.VMEM((PARTS, 16, TILE, WIDTH), BF16),
        pltpu.VMEM((PARTS, TILE, WIDTH), F32),
        pltpu.VMEM(slices, BF16),
        pltpu.VMEM(slices, BF16),
        pltpu.VMEM(half, BF16),
        pltpu.VMEM((FEATURES, FEATURES), F32),
        pltpu.VMEM((256, FEATURES), BF16),
        pltpu.VMEM((256, FEATURES), BF16),
        pltpu.VMEM((256, FEATURES), BF16),
        pltpu.VMEM((256, FEATURES), BF16),
        pltpu.VMEM((8, 16, FEATURES), F32),
        pltpu.VMEM((FEATURES, FEATURES), BF16),
    ]
    two = PARTS
    two = (PARTS,)
    sems = [
        (2,), (PARTS,),
        (4,), (4,), (4,), (4,), (1,),
        two, (PARTS, 8), two, (PARTS, 2), two, two,
        two, two, two, (8,),
        two, two, two, (PARTS, 8), two, two, two, two,
        (1,), (1,), (1,), (1,), (1,), (1,), (1,), (1,), (1,), (1,),
    ]
    activated, grad_input, grad_weight = pl.pallas_call(
        kernel,
        out_shape=(
            jax.ShapeDtypeStruct((ROWS, FEATURES), BF16),
            jax.ShapeDtypeStruct((ROWS, FEATURES), BF16),
            jax.ShapeDtypeStruct((FEATURES, FEATURES), BF16),
        ),
        in_specs=[hbm, hbm, hbm, smem, smem, hbm],
        out_specs=(hbm, hbm, hbm),
        scratch_shapes=scratch + [dma(n) for n in sems],
        compiler_params=pltpu.CompilerParams(
            collective_id=0, has_side_effects=True, vmem_limit_bytes=58 * 1024 * 1024
        ),
        cost_estimate=pl.CostEstimate(
            flops=10 * 2 * ROWS * ROWS * FEATURES, bytes_accessed=8 << 20, transcendentals=ROWS * FEATURES
        ),
    )(features, layer_weight, adjacency_tiles[0], tile_slots[0], tile_counts, cotangent)
    return hand_over(activated, grad_input, grad_weight)


def solution(mesh):
    return jax.shard_map(
        per_device,
        mesh=mesh,
        in_specs=(
            P("blk", None),
            P(),
            P("blk", "rep", None, None, None),
            P("blk", "rep", None),
            P("blk", "rep"),
            P("blk", None),
        ),
        out_specs=(P("blk", None), P("blk", None), P()),
        check_vma=False,
    )
```

```python
import math

import jax
import jax.numpy as jnp
from jax import lax
from jax.experimental import pallas as pl
from jax.experimental.pallas import tpu as pltpu
from jax.sharding import PartitionSpec as P

MESH = pl.DeviceIdType.MESH
F32, BF16 = jnp.float32, jnp.bfloat16
FEATURES = 512
TILE = 128
TILES = 8
SLOTS = 8
ROWS = 1024
GROUP = 256
GROUPS = ROWS // GROUP
PARTS = 4
WIDTH = FEATURES // PARTS
K0 = math.sqrt(2.0 / math.pi)
K1 = 0.044715


def tile_rows(t):
    return pl.ds(pl.multiple_of(t * TILE, TILE), TILE)


def group_rows(g):
    return pl.ds(pl.multiple_of(g * GROUP, GROUP), GROUP)


def part_rows(p):
    return pl.ds(pl.multiple_of(p * 16, 16), 16)


def columns_of(h):
    return pl.ds(h * WIDTH, WIDTH)


def remote(src, dst, send, recv, blk, rep):
    return pltpu.make_async_remote_copy(
        src_ref=src, dst_ref=dst, send_sem=send, recv_sem=recv,
        device_id=(blk, rep), device_id_type=MESH,
    )


def landed(dst, sem):
    pltpu.make_async_copy(dst, dst, sem).wait()


def dot(a, b):
    return jnp.dot(a, b, preferred_element_type=F32)


def kernel(
    feat, w_in, tiles, slots, counts, cot_in, act_out, gin, gw,
    w, wt, cot, act, tl, tt, inv, invv, invs, dense, denset, ring, blocks, acc, part, parts, agg, back,
    sib_out, sib_in, own_out, heap, total, hop_out, hop_in, grad,
    gw_part, gw_send, gw_recv, gw_half, gw_quarter, gw_ring, gw_fin,
    in_s, out_s,
    t_s, t_r, i_s, i_r, i_l, z_s, z_r, f_s, f_r, s_s, s_r, p_s, p_r, a_s, a_r,
    b_s, b_r, o_s, o_r, h_s, h_r, g_s, g_r,
    wx_s, wx_r, wq_s, wq_r, wz_s, wz_r, wf_s, wf_r, wy_s, wy_r,
):
    b = lax.axis_index("blk")
    r = lax.axis_index("rep")
    z, q = b // 4, b % 4
    yh, core = q // 2, q % 2
    me = yh * 8 + r
    sib = b + 1 - 2 * core
    up = ((z + 1) % 8) * 4 + q
    down = ((z + 7) % 8) * 4 + q
    mine = tile_rows(r)
    low, high = pl.ds(0, TILE // 2), pl.ds(TILE // 2, TILE // 2)

    def plane(y):
        return 4 * z + 2 * y + core

    def along(d):
        return ((z + d) % 8) * 4 + q

    barrier = pltpu.get_barrier_semaphore()
    pl.semaphore_signal(barrier, inc=1, device_id=(sib, r), device_id_type=MESH)

    @pl.loop(1, 8)
    def _(d):
        pl.semaphore_signal(barrier, inc=1, device_id=(along(d), r), device_id_type=MESH)

    @pl.loop(1, 16)
    def _(i):
        p = (me + i) % 16
        pl.semaphore_signal(barrier, inc=1, device_id=(plane(p // 8), p % 8), device_id_type=MESH)

    take_w = pltpu.make_async_copy(w_in, w, in_s.at[0])
    take_w.start()
    take_cot = pltpu.make_async_copy(cot_in, cot, in_s.at[1])
    take_cot.start()
    lane = lax.broadcasted_iota(jnp.int32, (8, TILE), 1)
    for s in range(4):
        index = jnp.full((8, TILE), SLOTS, jnp.int32)
        for k in range(SLOTS):
            index = jnp.where((lane == slots[s, k]) & (k < counts[0, s]), k, index)
        inv[s] = index
    pl.semaphore_wait(barrier, 23)

    sent = []

    def later(what, sem):
        sent.append(lambda: landed(what, sem))

    def peer(i):
        return (me + i) % 16

    def fellow(i):
        return (r + jnp.where(core == 0, i, 8 - i)) % 8

    def giver(i):
        return (r + jnp.where(core == 0, 8 - i, i)) % 8

    def own(h):
        return feat.at[mine, columns_of(h)]

    def shifted(d, y):
        return jnp.where((q == 3) & (y == 0), (d + 1) % 8, d)

    def spread(h, d):
        src = own(h) if d == 0 else ring.at[h, d]
        dst = blocks.at[h, q, mine]
        if d == 0:
            y = 1 - yh
            remote(src, dst, f_s.at[h], f_r.at[h, yh], plane(y), shifted(0, y)).start()

            @pl.when(r == 0)
            def _():
                pltpu.make_async_copy(
                    feat.at[:, columns_of(h)], blocks.at[h, q], f_r.at[h, yh]
                ).start()

            return
        for y in range(2):
            to = shifted(d, y)
            here = (yh == y) & (r == to)

            @pl.when(here)
            def _():
                pltpu.make_async_copy(src, dst, f_r.at[h, yh]).start()

            @pl.when(jnp.logical_not(here))
            def _():
                remote(src, dst, f_s.at[h], f_r.at[h, yh], plane(y), to).start()

    for h in range(PARTS):
        remote(own(h), ring.at[h, 1], z_s.at[h], z_r.at[h, 1], down, r).start()
        remote(own(h), ring.at[h, 7], z_s.at[h], z_r.at[h, 7], up, r).start()
    for m in range(4):
        off = q - 2 + m
        turn = jnp.where(off < -1, -1, jnp.where(off >= 4, 1, 0))
        slot = (off + 4) % 4
        to = (r + turn + 8) % 8

        @pl.when(turn == 0)
        def _():
            pltpu.make_async_copy(tiles.at[m], tl.at[slot, pl.ds(0, SLOTS)], t_r.at[slot]).start()
            pltpu.make_async_copy(inv.at[m], invv.at[slot], i_r.at[slot]).start()

        @pl.when(turn != 0)
        def _():
            remote(tiles.at[m], tl.at[slot, pl.ds(0, SLOTS)], t_s.at[m], t_r.at[slot], b, to).start()
            remote(inv.at[m], invv.at[slot], i_s.at[m], i_r.at[slot], b, to).start()

    def forward_ring(h, k):
        landed(ring.at[h, k], z_r.at[h, k])
        landed(ring.at[h, 8 - k], z_r.at[h, 8 - k])
        if k < 3:
            remote(ring.at[h, k], ring.at[h, k + 1], z_s.at[h], z_r.at[h, k + 1], down, r).start()
            remote(ring.at[h, 8 - k], ring.at[h, 7 - k], z_s.at[h], z_r.at[h, 7 - k], up, r).start()
        else:
            remote(ring.at[h, 3, low], ring.at[h, 4, low], z_s.at[h], z_r.at[h, 4], down, r).start()
            remote(ring.at[h, 5, high], ring.at[h, 4, high], z_s.at[h], z_r.at[h, 0], up, r).start()

    def last_of_ring(h):
        landed(ring.at[h, 4, low], z_r.at[h, 4])
        landed(ring.at[h, 4, high], z_r.at[h, 0])

    for turn in range(PARTS + 4):
        for h in range(PARTS):
            k = turn - h
            if k == 0:
                spread(h, 0)
            elif 1 <= k <= 3:
                forward_ring(h, k)
                spread(h, k)
                spread(h, 8 - k)
            elif k == 4:
                last_of_ring(h)
                spread(h, 4)
    for h in range(PARTS):
        later(ring.at[h, pl.ds(0, 7)], z_s.at[h])

    def features_sent():
        for count, which in ((15, r == 0), (14, r != 0)):
            @pl.when(which)
            def _():
                for h in range(PARTS):
                    landed(heap.at[h, pl.ds(0, count)], f_s.at[h])

    sent.append(features_sent)

    def lists_sent():
        for m in range(4):
            off = q - 2 + m

            @pl.when((off < -1) | (off >= 4))
            def _():
                landed(tiles.at[m], t_s.at[m])
                landed(inv.at[m], i_s.at[m])

    sent.append(lists_sent)
    take_w.wait()
    wt[...] = w[...].T
    for s in range(4):
        landed(tl.at[s, pl.ds(0, SLOTS)], t_r.at[s])
        landed(invv.at[s], i_r.at[s])
    move = pltpu.make_async_copy(invv, invs, i_l.at[0])
    move.start()
    zero = jnp.zeros((TILE, TILE), BF16)
    for s in range(4):
        tl[s, SLOTS] = zero
        tt[s, SLOTS] = zero

    move.wait()

    def build(first):
        @pl.loop(0, 2 * TILES)
        def _(i):
            s, t = first + 2 * (i // TILES), i % TILES
            for c in range(TILES):
                dense[s, tile_rows(t), c * TILE:(c + 1) * TILE] = tl[s, invs[s, 0, t * TILES + c]]

    build(core)

    def transpose_list(s):
        @pl.loop(0, SLOTS)
        def _(i):
            tt[s, i] = tl[s, i].T

        @pl.loop(0, TILES)
        def _(t):
            for c in range(TILES):
                denset[s, tile_rows(t), c * TILE:(c + 1) * TILE] = tt[s, invs[s, 0, c * TILES + t]]

    take_cot.wait()

    def pass_on(h):
        for y in range(2):
            piece = blocks.at[h, 2 * y + core]
            landed(piece, f_r.at[h, y])
            remote(piece, piece, s_s.at[h], s_r.at[h], sib, r).start()

        later(heap.at[h], s_s.at[h])

    def own_blocks(h):
        @pl.loop(0, GROUPS)
        def _(g):
            rows = group_rows(g)
            acc[h, rows] = dot(dense[core, rows, :], blocks[h, core]) + dot(
                dense[2 + core, rows, :], blocks[h, 2 + core]
            )

    def sibling_blocks(h):
        landed(heap.at[h], s_r.at[h])

        @pl.loop(0, GROUPS)
        def _(i):
            g = (r // 2 + jnp.where(core == 0, 1 + i, 3 - i)) % GROUPS
            rows = group_rows(g)
            value = dot(dense[1 - core, rows, :], blocks[h, 1 - core]) + dot(
                dense[3 - core, rows, :], blocks[h, 3 - core]
            )
            part[h, rows] = (acc[h, rows] + value).astype(BF16)
            for j in range(2):
                t = 2 * g + j

                @pl.when(t != r)
                def _():
                    remote(part.at[h, tile_rows(t)], parts.at[h, r], p_s.at[h], p_r.at[h], b, t).start()

        later(parts.at[h, pl.ds(0, 7)], p_s.at[h])

    def add_parts(h):
        landed(parts.at[h, pl.ds(0, 7)], p_r.at[h])
        acc[h, 0:TILE] = part[h, mine].astype(F32)

        @pl.loop(1, 8)
        def _(i):
            acc[h, 0:TILE] += parts[h, giver(i)].astype(F32)

        agg[h, mine] = acc[h, 0:TILE].astype(BF16)

    def share(h):
        @pl.loop(1, 8)
        def _(i):
            t = fellow(i)
            remote(agg.at[h, mine], agg.at[h, mine], a_s.at[h], a_r.at[r], b, t).start()

        later(parts.at[h, pl.ds(0, 7)], a_s.at[h])

    for h in range(PARTS):
        if h > 0:
            transpose_list(h - 1)
        pass_on(h)
        own_blocks(h)
        if h == 0:
            build(1 - core)
        sibling_blocks(h)
        if h >= 2:
            add_parts(h - 2)
            share(h - 2)
    for h in range(PARTS - 2, PARTS):
        add_parts(h)
        share(h)
    transpose_list(3)

    def chunk(c):
        rows = tile_rows(c)
        inputs = jnp.concatenate([agg[h, rows] for h in range(PARTS)], axis=1)
        pre = dot(inputs, w[...])
        square = pre * pre
        t = jnp.tanh(K0 * (pre + K1 * square * pre))
        half = 0.5 * (1.0 + t)
        act[rows] = (pre * half).astype(BF16)
        pltpu.make_async_copy(act.at[rows], act_out.at[rows], out_s.at[0]).start()
        slope = half + 0.5 * pre * (1.0 - t * t) * (K0 * (1.0 + 3.0 * K1 * square))
        delta = (cot[rows].astype(F32) * slope).astype(BF16)
        value = dot(delta, wt[...]).astype(BF16)
        for h in range(PARTS):
            back[h, rows] = value[:, h * WIDTH:(h + 1) * WIDTH]
        return inputs, delta

    gw_part[...] = lax.dot_general(
        *chunk(r), (((0,), (0,)), ((), ())), preferred_element_type=F32
    )
    gw_send[...] = gw_part[group_rows(1 - core)].astype(BF16)
    remote(gw_send, gw_recv, wx_s.at[0], wx_r.at[0], sib, r).start()
    later(gw_send, wx_s.at[0])

    @pl.loop(1, 8)
    def _(i):
        c = giver(i)
        landed(agg.at[0, pl.ds(0, PARTS * TILE)], a_r.at[c])
        chunk(c)

    landed(gw_recv, wx_r.at[0])
    gw_half[...] = (gw_part[group_rows(core)] + gw_recv[...].astype(F32)).astype(BF16)

    @pl.loop(1, 16)
    def _(i):
        p = (me + i) % 16
        remote(
            gw_half.at[part_rows(p)], gw_quarter.at[part_rows(me)], wq_s.at[0], wq_r.at[0],
            plane(p // 8), p % 8,
        ).start()

    later(gw_half.at[pl.ds(0, 240)], wq_s.at[0])
    def side_by_side(ref, pair, *at):
        return jnp.concatenate([ref[(2 * pair, *at)], ref[(2 * pair + 1, *at)]], axis=1)

    def sibling_grads(pair):
        @pl.loop(0, 2 * GROUPS)
        def _(i):
            y, g = i // GROUPS, i % GROUPS
            rows = group_rows(g)
            value = dot(denset[2 * y + 1 - core, rows, :], side_by_side(back, pair)).astype(BF16)
            for n in range(2):
                h = 2 * pair + n
                sib_out[h, y, rows] = value[:, n * WIDTH:(n + 1) * WIDTH]
                remote(
                    sib_out.at[h, y, rows], sib_in.at[h, y, rows], b_s.at[h], b_r.at[h], sib, r
                ).start()

        for n in range(2):
            later(sib_out.at[2 * pair + n], b_s.at[2 * pair + n])

    def own_grads(pair):
        for n in range(2):
            landed(sib_in.at[2 * pair + n], b_r.at[2 * pair + n])

        @pl.loop(0, 2 * GROUPS)
        def _(i):
            j = i % 4
            y, g = (i + i // 4) % 2, (r // 2 + 2 * j + 1 + 5 * (j // 2)) % GROUPS
            rows = group_rows(g)
            value = dot(denset[2 * y + core, rows, :], side_by_side(back, pair))
            turned = jnp.where((yh == 0) & (core == 1) & (y == 1), (r + 7) % 8, r)
            for n in range(2):
                h = 2 * pair + n
                own_out[h, y, rows] = (
                    value[:, n * WIDTH:(n + 1) * WIDTH] + sib_in[h, y, rows].astype(F32)
                ).astype(BF16)
                for j in range(2):
                    t = 2 * g + j
                    src, dst = own_out.at[h, y, tile_rows(t)], heap.at[h, me]
                    here = (yh == y) & (r == t)

                    @pl.when(here)
                    def _():
                        pltpu.make_async_copy(src, dst, o_r.at[h, turned]).start()

                    @pl.when(jnp.logical_not(here))
                    def _():
                        remote(src, dst, o_s.at[h], o_r.at[h, turned], plane(y), t).start()

        for n in range(2):
            later(heap.at[0, pl.ds(0, 15)], o_s.at[2 * pair + n])

    sibling_grads(0)
    sibling_grads(1)
    own_grads(0)
    own_grads(1)
    landed(gw_quarter.at[pl.ds(0, 240)], wq_r.at[0])
    gw_ring[0] = gw_half[part_rows(me)].astype(F32)

    @pl.loop(1, 16)
    def _(i):
        p = (me + i) % 16
        gw_ring[0] += gw_quarter[part_rows(p)].astype(F32)

    @pl.loop(1, 8)
    def _(d):
        remote(gw_ring.at[0], gw_ring.at[d], wz_s.at[0], wz_r.at[0], along(d), r).start()

    later(gw_ring.at[pl.ds(0, 7)], wz_s.at[0])

    def send_along(h):
        @pl.loop(0, 8)
        def _(i):
            d = 2 * ((r // 2 + 7 - i // 2 - 2 * yh) % 4) + i % 2
            first = shifted(d, 0)
            landed(heap.at[h, pl.ds(0, 2)], o_r.at[h, d])
            value = heap[h, first].astype(F32) + heap[h, 8 + d].astype(F32)

            @pl.when(d == 0)
            def _():
                total[h] = value

            @pl.when(d != 0)
            def _():
                hop_out[h, d] = value.astype(BF16)
                remote(hop_out.at[h, d], hop_in.at[h, d], h_s.at[h], h_r.at[h], along(d), r).start()

        later(ring.at[h, pl.ds(0, 7)], h_s.at[h])

    def finish(h):
        landed(hop_in.at[h, pl.ds(0, 7)], h_r.at[h])

        @pl.loop(1, 8)
        def _(d):
            total[h] += hop_in[h, d].astype(F32)

        place = grad.at[h, mine]
        grad[h, mine] = total[h].astype(BF16)

        @pl.loop(1, 8)
        def _(i):
            t = fellow(i)
            remote(place, place, g_s.at[h], g_r.at[h], b, t).start()

        later(parts.at[h, pl.ds(0, 7)], g_s.at[h])

    send_along(0)
    send_along(1)
    landed(gw_ring.at[pl.ds(0, 7)], wz_r.at[0])

    whole = gw_ring[z]
    for k in range(1, 8):
        whole = whole + gw_ring[(z + 8 - k) % 8]
    place = pl.ds(pl.multiple_of(core * 256 + me * 16, 16), 16)
    gw_fin[place] = (whole * (1.0 / math.sqrt(32 * ROWS))).astype(BF16)

    @pl.loop(1, 16)
    def _(i):
        p = (me + i) % 16
        remote(
            gw_fin.at[place], gw_fin.at[place], wf_s.at[0], wf_r.at[0], plane(p // 8), p % 8
        ).start()

    later(gw_half.at[pl.ds(0, 240)], wf_s.at[0])

    for h in range(PARTS):
        finish(h)
        if h + 2 < PARTS:
            send_along(h + 2)

    landed(gw_fin.at[pl.ds(0, 240)], wf_r.at[0])
    landed(act, out_s.at[0])

    half = group_rows(core)
    remote(gw_fin.at[half], gw_fin.at[half], wy_s.at[0], wy_r.at[0], sib, r).start()
    later(gw_fin.at[half], wy_s.at[0])
    landed(gw_fin.at[group_rows(1 - core)], wy_r.at[0])
    give_gw = pltpu.make_async_copy(gw_fin, gw, in_s.at[0])
    give_gw.start()

    for h in range(PARTS):
        landed(parts.at[h, pl.ds(0, 7)], g_r.at[h])
        pltpu.make_async_copy(grad.at[h], gin.at[:, columns_of(h)], out_s.at[h]).start()

    for wait in sent:
        wait()
    give_gw.wait()
    for h in range(PARTS):
        landed(grad.at[h], out_s.at[h])


def hand_over_kernel(act, grad, weight, act_out, grad_out, weight_out, held, narrow, wide, get, give):
    rows = ROWS // 4
    gets, gives = [], []
    for n, (src, dst) in enumerate(((act, act_out), (grad, grad_out))):
        for m in range(4):
            part, place = pl.ds(m * rows, rows), held.at[4 * n + m]
            gets.append(pltpu.make_async_copy(src.at[part], place, get.at[4 * n + m]))
            gives.append(pltpu.make_async_copy(place, dst.at[part], give.at[4 * n + m]))
    take = pltpu.make_async_copy(weight, narrow, get.at[8])
    take.start()
    for copy in gets:
        copy.start()
    take.wait()
    wide[...] = narrow[...].astype(F32)
    put = pltpu.make_async_copy(wide, weight_out, give.at[8])
    put.start()
    for first, second in zip(gets, gives):
        first.wait()
        second.start()
    for copy in gives:
        copy.wait()
    put.wait()


def hand_over(act, grad, weight):
    hbm = pl.BlockSpec(memory_space=pl.ANY)
    return pl.pallas_call(
        hand_over_kernel,
        out_shape=(
            jax.ShapeDtypeStruct((ROWS, FEATURES), BF16),
            jax.ShapeDtypeStruct((ROWS, FEATURES), BF16),
            jax.ShapeDtypeStruct((FEATURES, FEATURES), F32),
        ),
        in_specs=[hbm, hbm, hbm],
        out_specs=(hbm, hbm, hbm),
        scratch_shapes=[
            pltpu.VMEM((8, ROWS // 4, FEATURES), BF16),
            pltpu.VMEM((FEATURES, FEATURES), BF16),
            pltpu.VMEM((FEATURES, FEATURES), F32),
            pltpu.SemaphoreType.DMA((9,)),
            pltpu.SemaphoreType.DMA((9,)),
        ],
        compiler_params=pltpu.CompilerParams(vmem_limit_bytes=60 * 1024 * 1024),
        cost_estimate=pl.CostEstimate(flops=0, bytes_accessed=6 << 20, transcendentals=0),
    )(act, grad, weight)


def per_device(features, layer_weight, adjacency_tiles, tile_slots, tile_counts, cotangent):
    hbm = pl.BlockSpec(memory_space=pl.ANY)
    smem = pl.BlockSpec(memory_space=pltpu.SMEM)
    dma = pltpu.SemaphoreType.DMA
    half = (PARTS, ROWS, WIDTH)
    slices = (PARTS, 8, TILE, WIDTH)
    scratch = [
        pltpu.VMEM((FEATURES, FEATURES), BF16),
        pltpu.VMEM((FEATURES, FEATURES), BF16),
        pltpu.VMEM((ROWS, FEATURES), BF16),
        pltpu.VMEM((ROWS, FEATURES), BF16),
        pltpu.VMEM((4, SLOTS + 1, TILE, TILE), BF16),
        pltpu.VMEM((4, SLOTS + 1, TILE, TILE), BF16),
        pltpu.VMEM((4, 8, TILE), jnp.int32),
        pltpu.VMEM((4, 8, TILE), jnp.int32),
        pltpu.SMEM((4, 8, TILE), jnp.int32),
        pltpu.VMEM((4, ROWS, ROWS), BF16),
        pltpu.VMEM((4, ROWS, ROWS), BF16),
        pltpu.VMEM(slices, BF16),
        pltpu.VMEM((PARTS, 4, ROWS, WIDTH), BF16),
        pltpu.VMEM(half, F32),
        pltpu.VMEM(half, BF16),
        pltpu.VMEM(slices, BF16),
        pltpu.VMEM(half, BF16),
        pltpu.VMEM(half, BF16),
        pltpu.VMEM((PARTS, 2, ROWS, WIDTH), BF16),
        pltpu.VMEM((PARTS, 2, ROWS, WIDTH), BF16),
        pltpu.VMEM((PARTS, 2, ROWS, WIDTH), BF16),
        pltpu.VMEM((PARTS, 16, TILE, WIDTH), BF16),
        pltpu.VMEM((PARTS, TILE, WIDTH), F32),
        pltpu.VMEM(slices, BF16),
        pltpu.VMEM(slices, BF16),
        pltpu.VMEM(half, BF16),
        pltpu.VMEM((FEATURES, FEATURES), F32),
        pltpu.VMEM((256, FEATURES), BF16),
        pltpu.VMEM((256, FEATURES), BF16),
        pltpu.VMEM((256, FEATURES), BF16),
        pltpu.VMEM((256, FEATURES), BF16),
        pltpu.VMEM((8, 16, FEATURES), F32),
        pltpu.VMEM((FEATURES, FEATURES), BF16),
    ]
    two = PARTS
    two = (PARTS,)
    sems = [
        (2,), (PARTS,),
        (4,), (4,), (4,), (4,), (1,),
        two, (PARTS, 8), two, (PARTS, 2), two, two,
        two, two, two, (8,),
        two, two, two, (PARTS, 8), two, two, two, two,
        (1,), (1,), (1,), (1,), (1,), (1,), (1,), (1,), (1,), (1,),
    ]
    activated, grad_input, grad_weight = pl.pallas_call(
        kernel,
        out_shape=(
            jax.ShapeDtypeStruct((ROWS, FEATURES), BF16),
            jax.ShapeDtypeStruct((ROWS, FEATURES), BF16),
            jax.ShapeDtypeStruct((FEATURES, FEATURES), BF16),
        ),
        in_specs=[hbm, hbm, hbm, smem, smem, hbm],
        out_specs=(hbm, hbm, hbm),
        scratch_shapes=scratch + [dma(n) for n in sems],
        compiler_params=pltpu.CompilerParams(
            collective_id=0, has_side_effects=True, vmem_limit_bytes=58 * 1024 * 1024
        ),
        cost_estimate=pl.CostEstimate(
            flops=10 * 2 * ROWS * ROWS * FEATURES, bytes_accessed=8 << 20, transcendentals=ROWS * FEATURES
        ),
    )(features, layer_weight, adjacency_tiles[0], tile_slots[0], tile_counts, cotangent)
    return hand_over(activated, grad_input, grad_weight)


def solution(mesh):
    return jax.shard_map(
        per_device,
        mesh=mesh,
        in_specs=(
            P("blk", None),
            P(),
            P("blk", "rep", None, None, None),
            P("blk", "rep", None),
            P("blk", "rep"),
            P("blk", None),
        ),
        out_specs=(P("blk", None), P("blk", None), P()),
        check_vma=False,
    )
```
